256 devices in a mesh: band: 128 (over z, x, y), mp: 2 (over core).
Axes of the slice: x: 4, y: 4, z: 8, core: 2. Of those that a mesh axis runs over, the one named last changes fastest.
Arguments:
- grid: bfloat16 [163840, 512], P('band', 'mp'), may hold values from -6 to 6
- interp: bfloat16 [1280, 4, 128, 128], P('band'), may hold values from -0.5 to 0.5
- mesh_init: bfloat16 [32768, 512], P('band', 'mp'), may hold values from -6 to 6
- w_enc: bfloat16 [512, 512], P(None, 'mp'), may hold values from -0.25 to 0.25
- w_dec: bfloat16 [512, 512], P(None, 'mp'), may hold values from -0.25 to 0.25
- cotangent: bfloat16 [163840, 512], P('band', 'mp'), may hold values from -6 to 6
- pair_mesh: int32 [1280, 4], P('band'), may hold values from 0 to 255, as said below
- pair_count: int32 [1280], P('band'), may hold values from 2 to 4, as said below
Outputs:
- grid_out: bfloat16 [163840, 512], P('band', 'mp')
- grad_enc: float32 [512, 512], P(None, 'mp')
- grad_dec: float32 [512, 512], P(None, 'mp')
The draws below stay inside these ranges and needn't reach their ends.
Inputs may be any that keep to these rules, and one draw needn't show every extreme that they name: The owner of mesh block pair_mesh[b, k], device pair_mesh[b, k] // 2 of band, lies at most 2 devices from grid block b's device b // 10; in every band some slot reaches 2 devices up and some 2 devices down, where such devices exist. Slots k < pair_count[b] of grid block b are used, the others are not.
All inputs are finite; a program needn't handle non-finite values.
Results may differ from the reference program's by a relative error of at most 0.0075.
Values may be sent and summed in bfloat16 or wider, within the bound.
No kernel may reach another device: no remote copies, remote signals or barrier semaphores. Data moves between devices by JAX's collectives and lax.ppermute only.
A program may use at most 128 MiB of HBM per device.

```python
import jax
import jax.numpy as jnp
from jax import lax

L = 512
GB = 128
MBR = 128
K = 4
REACH = 2
NBLK_DEV = 10
MB_DEV = 2
NBLK = 1280
NMB = 256
NG = 163840
NM = 32768
N_BAND = 128


def draw_pair_mesh(key, part):
    key = jax.random.fold_in(key, 7)
    band_count = NBLK // NBLK_DEV
    block_ids = jnp.arange(NBLK)
    device_ids = block_ids // NBLK_DEV
    offsets = jax.random.randint(key, (NBLK, K), -REACH, REACH + 1)
    chosen_block = jax.random.randint(jax.random.fold_in(key, 1), (band_count,), 0, NBLK_DEV)
    chosen_slot = jax.random.randint(jax.random.fold_in(key, 2), (band_count,), 0, K)
    is_block = (block_ids % NBLK_DEV == chosen_block[device_ids])[:, None]
    slot_ids = jnp.arange(K)[None, :]
    upper_slot = chosen_slot[device_ids][:, None]
    offsets = jnp.where(is_block & (slot_ids == upper_slot), REACH, offsets)
    offsets = jnp.where(is_block & (slot_ids == (upper_slot + 1) % K), -REACH, offsets)
    owners = jnp.clip(device_ids[:, None] + offsets, 0, band_count - 1)
    within = jax.random.randint(jax.random.fold_in(key, 3), (NBLK, K), 0, MB_DEV)
    return (owners * MB_DEV + within).astype(jnp.int32)


def draw_pair_count(key, part):
    key = jax.random.fold_in(key, 13)
    band_count = NBLK // NBLK_DEV
    device_ids = jnp.arange(NBLK) // NBLK_DEV
    distance = jnp.abs(2 * device_ids - (band_count - 1))
    base_count = 2 + (K - 2) * distance // max(band_count - 1, 1)
    jitter = jax.random.randint(key, (NBLK,), -1, 1)
    counts = jnp.clip(base_count + jitter, 2, K)
    picked = jax.random.randint(jax.random.fold_in(key, 1), (), 0, NBLK_DEV)
    counts = jnp.where(jnp.arange(NBLK) == picked, K, counts)
    return counts.astype(jnp.int32)


def shard_levels(key, extent, pieces, least, largest):
    loudness = 1.0
    for axis_at, shards_of in pieces:
        draws = jax.random.uniform(jax.random.fold_in(jax.random.fold_in(key, 6), axis_at), (shards_of,), jnp.float32, least / len(pieces), largest / len(pieces))
        loudness = loudness * jnp.repeat(jnp.exp(draws), extent[axis_at] // shards_of).reshape((-1,) + (1,) * (len(extent) - 1 - axis_at))
    return loudness


def normal_values(stream_key, extent, width, reach, cuts=(), kind=jnp.bfloat16):
    level = shard_levels(stream_key, extent, cuts, -0.22, 0.18) if cuts else 1.0
    result = jax.random.normal(stream_key, extent, jnp.float32) * width * level
    return jnp.minimum(jnp.maximum(result, -reach), reach).astype(kind)


def setup_inputs(seed: int = 0) -> dict:
    streams_of = jax.random.split(jax.random.key(seed), 9)
    grid = normal_values(streams_of[0], (NG, L), 1.0, 6.0, ((0, 128), (1, 2)))
    interp = normal_values(streams_of[1], (NBLK, K, MBR, GB), GB ** -0.5, 0.5, ((0, 128),))
    mesh_init = normal_values(streams_of[2], (NM, L), 1.0, 6.0, ((0, 128), (1, 2)))
    w_enc = normal_values(streams_of[3], (L, L), L ** -0.5, 0.25, ((1, 2),))
    w_dec = normal_values(streams_of[4], (L, L), L ** -0.5, 0.25, ((1, 2),))
    cotangent = normal_values(streams_of[5], (NG, L), 1.0, 6.0, ((0, 128), (1, 2)))
    pair_mesh = draw_pair_mesh(jax.random.fold_in(streams_of[8], 71), 0)
    pair_count = draw_pair_count(jax.random.fold_in(streams_of[8], 71), 0)
    return {"grid": grid, "interp": interp, "mesh_init": mesh_init, "w_enc": w_enc, "w_dec": w_dec, "cotangent": cotangent, "pair_mesh": pair_mesh, "pair_count": pair_count}


def silu_slope(pre, sig):
    return sig * (1.0 + pre * (1.0 - sig))


def reference(grid, interp, mesh_init, w_enc, w_dec, cotangent, pair_mesh, pair_count):
    fl = jnp.float32
    group_pairs = NBLK_DEV * K
    live_mask = (jnp.arange(K)[None, :] < pair_count[:, None]).astype(fl)
    grid_groups = grid.reshape(N_BAND, NBLK_DEV, GB, L)
    interp_groups = interp.reshape(N_BAND, NBLK_DEV, K, MBR, GB)
    mesh_groups = pair_mesh.reshape(N_BAND, group_pairs).astype(jnp.int32)
    live_groups = live_mask.reshape(N_BAND, group_pairs, 1, 1)
    cot_groups = cotangent.reshape(N_BAND, NBLK_DEV, GB, L)

    def encode(grid_blocks, weights):
        messages = jnp.einsum('bkrg,bgf->bkrf', weights.astype(fl), grid_blocks.astype(fl))
        messages = messages.astype(jnp.bfloat16).reshape(group_pairs, MBR, L)
        pre = jnp.dot(messages.reshape(group_pairs * MBR, L), w_enc, preferred_element_type=fl)
        return messages, pre.reshape(group_pairs, MBR, L)

    def enc_step(total, inputs):
        grid_blocks, weights, targets, live = inputs
        messages, pre = encode(grid_blocks, weights)
        edge_out = pre * jax.nn.sigmoid(pre) * live
        return total.at[targets].add(edge_out), None

    agg, unused = lax.scan(enc_step, jnp.zeros((NMB, MBR, L), fl),
                           (grid_groups, interp_groups, mesh_groups, live_groups))
    mesh_lat = (mesh_init.astype(fl).reshape(NMB, MBR, L) + 0.25 * agg).astype(jnp.bfloat16)

    def dec_step(carry, inputs):
        lift_total, grad_dec = carry
        grid_blocks, weights, targets, live, upstream = inputs
        flat_weights = weights.reshape(group_pairs, MBR, GB)
        chosen = mesh_lat[targets]
        decoded = jnp.einsum('prg,prf->pgf', flat_weights.astype(fl), chosen.astype(fl)).astype(jnp.bfloat16)
        pre = jnp.dot(decoded.reshape(group_pairs * GB, L), w_dec, preferred_element_type=fl)
        pre = pre.reshape(group_pairs, GB, L)
        sig = jax.nn.sigmoid(pre)
        node_out = (pre * sig * live).reshape(NBLK_DEV, K, GB, L).sum(axis=1)
        out_blocks = (grid_blocks.astype(fl) + node_out).astype(jnp.bfloat16)
        slope = (silu_slope(pre, sig) * live).reshape(NBLK_DEV, K, GB, L)
        grad_pre = (upstream.astype(fl)[:, None] * slope).astype(jnp.bfloat16).reshape(group_pairs, GB, L)
        grad_dec = grad_dec + jnp.einsum('pgf,pgh->fh', decoded.astype(fl), grad_pre.astype(fl))
        lifted = jnp.einsum('prg,pgh->prh', flat_weights.astype(fl), grad_pre.astype(fl))
        return (lift_total.at[targets].add(lifted), grad_dec), out_blocks

    (lift_total, grad_dec), out_groups = lax.scan(
        dec_step, (jnp.zeros((NMB, MBR, L), fl), jnp.zeros((L, L), fl)),
        (grid_groups, interp_groups, mesh_groups, live_groups, cot_groups))
    grad_mesh = jnp.dot(lift_total.reshape(NM, L), w_dec.astype(fl).T,
                        precision=lax.Precision.HIGHEST).reshape(NMB, MBR, L)

    def genc_step(grad_enc, inputs):
        grid_blocks, weights, targets, live = inputs
        messages, pre = encode(grid_blocks, weights)
        sig = jax.nn.sigmoid(pre)
        grad_edge = (0.25 * grad_mesh[targets] * silu_slope(pre, sig) * live).astype(jnp.bfloat16)
        return grad_enc + jnp.einsum('prf,prh->fh', messages.astype(fl), grad_edge.astype(fl)), None

    grad_enc, unused = lax.scan(genc_step, jnp.zeros((L, L), fl),
                                (grid_groups, interp_groups, mesh_groups, live_groups))
    return out_groups.reshape(NG, L), grad_enc, grad_dec
```

```python
import jax
import jax.numpy as jnp
from jax import lax
from jax.sharding import PartitionSpec as P

REACH = 2


def shifted(value, axis, steps):
    count = lax.axis_size(axis)
    first, last = (max(0, -steps), min(count, count - steps))
    return lax.ppermute(value, axis, [(source, source + steps) for source in range(first, last)])


def silu_slope(pre, sig):
    return sig * (1.0 + pre * (1.0 - sig))


def halves(value):
    width = value.shape[1] // 2
    return [value[:, :width], value[:, width:]]


def band_sum(values):
    fl, bf = jnp.float32, jnp.bfloat16
    count = lax.axis_size("band")
    rows, width = values[0].shape
    flat = jnp.concatenate([half for value in values for half in halves(value)], axis=0)
    chunks = flat.astype(bf).reshape(count, -1, width // 2)
    parts = lax.all_to_all(chunks, "band", 0, 0, tiled=True)
    total = parts.astype(fl).sum(axis=0).astype(bf)
    spread = jnp.broadcast_to(total[None], parts.shape)
    flat = lax.all_to_all(spread, "band", 0, 0, tiled=True).reshape(-1, rows, width // 2)
    flat = flat.astype(fl)
    return [jnp.concatenate([flat[2 * i], flat[2 * i + 1]], axis=1) for i in range(len(values))]


def local(grid, interp, mesh_init, w_enc, w_dec, cotangent, pair_mesh, pair_count):
    fl, bf = jnp.float32, jnp.bfloat16
    blocks, pair_slots, mesh_rows, block_rows = interp.shape
    half_width = grid.shape[1]
    full_width = w_enc.shape[0]
    count_pairs = blocks * pair_slots
    reach_devs = REACH
    slab_count = 2 * reach_devs + 1
    owner_rows = mesh_init.shape[0]
    owner_blocks = owner_rows // mesh_rows
    slot_total = slab_count * owner_blocks
    offsets = [offset for offset in range(-reach_devs, reach_devs + 1) if offset != 0]
    band_index = lax.axis_index("band")
    targets = pair_mesh.reshape(count_pairs)
    slot_index = (
        targets // owner_blocks - band_index + reach_devs
    ) * owner_blocks + targets % owner_blocks
    onehot = (slot_index[None, :] == jnp.arange(slot_total)[:, None]).astype(fl)
    live_mask = (jnp.arange(pair_slots)[None, :] < pair_count[:, None]).astype(fl)
    live_pairs = live_mask.reshape(count_pairs, 1, 1)
    weights = interp.reshape(count_pairs, mesh_rows, block_rows)
    grid_full = lax.all_gather(grid, "mp", axis=1, tiled=True)
    messages = jnp.einsum(
        "bkrg,bgf->bkrf",
        interp,
        grid_full.reshape(blocks, block_rows, full_width),
        preferred_element_type=fl,
    ).astype(bf)
    messages = messages.reshape(count_pairs, mesh_rows, full_width)
    pre_enc = jnp.dot(
        messages.reshape(count_pairs * mesh_rows, full_width), w_enc, preferred_element_type=fl
    ).reshape(count_pairs, mesh_rows, half_width)
    sig_enc = jax.nn.sigmoid(pre_enc)
    edge_out = pre_enc * sig_enc * live_pairs
    slabs = jnp.einsum("sp,prh->srh", onehot, edge_out, precision=lax.Precision.HIGHEST)
    slabs = slabs.reshape(slab_count, owner_rows, half_width)
    aggregate = slabs[reach_devs]
    for offset in offsets:
        sent = slabs[reach_devs + offset].astype(bf)
        aggregate = aggregate + shifted(sent, "band", offset).astype(fl)
    mesh_lat = (mesh_init.astype(fl) + 0.25 * aggregate).astype(bf)
    pieces = []
    for offset in range(-reach_devs, reach_devs + 1):
        if offset == 0:
            pieces.append(mesh_lat)
        else:
            pieces.append(shifted(mesh_lat, "band", -offset))
    nearby = lax.all_gather(jnp.concatenate(pieces, axis=0), "mp", axis=1, tiled=True)
    nearby = nearby.reshape(slot_total, mesh_rows, full_width)
    chosen = jnp.take(nearby, slot_index, axis=0)
    decoded = jnp.einsum("prg,prf->pgf", weights, chosen, preferred_element_type=fl).astype(bf)
    pre_dec = jnp.dot(
        decoded.reshape(count_pairs * block_rows, full_width), w_dec, preferred_element_type=fl
    ).reshape(count_pairs, block_rows, half_width)
    sig_dec = jax.nn.sigmoid(pre_dec)
    node_out = (
        (pre_dec * sig_dec * live_pairs)
        .reshape(blocks, pair_slots, block_rows, half_width)
        .sum(axis=1)
    )
    grid_out = grid.astype(fl).reshape(blocks, block_rows, half_width) + node_out
    grid_out = grid_out.reshape(blocks * block_rows, half_width).astype(bf)
    upstream = cotangent.astype(fl).reshape(blocks, 1, block_rows, half_width)
    slope_dec = (silu_slope(pre_dec, sig_dec) * live_pairs).reshape(
        blocks, pair_slots, block_rows, half_width
    )
    grad_pre = (upstream * slope_dec).astype(bf).reshape(count_pairs, block_rows, half_width)
    grad_dec = jnp.einsum("pgf,pgh->fh", decoded, grad_pre, preferred_element_type=fl)
    lifted = jnp.einsum("prg,pgh->prh", weights, grad_pre, preferred_element_type=fl)
    grad_slabs = jnp.einsum("sp,prh->srh", onehot, lifted, precision=lax.Precision.HIGHEST)
    grad_slabs = grad_slabs.reshape(slab_count, owner_rows, half_width)
    collected = grad_slabs[reach_devs]
    for offset in offsets:
        sent = grad_slabs[reach_devs + offset].astype(bf)
        collected = collected + shifted(sent, "band", offset).astype(fl)
    w_dec_full = lax.all_gather(w_dec, "mp", axis=1, tiled=True)
    mesh_half = w_dec_full.reshape(2, -1, full_width)
    w_rows = lax.dynamic_index_in_dim(mesh_half, lax.axis_index("mp"), 0, keepdims=False)
    lift = lax.all_gather(collected.astype(bf), "mp", axis=1, tiled=True)
    grad_mesh = jnp.dot(lift, w_rows.T, preferred_element_type=fl).astype(bf)
    grad_pieces = []
    for offset in range(-reach_devs, reach_devs + 1):
        if offset == 0:
            grad_pieces.append(grad_mesh)
        else:
            grad_pieces.append(shifted(grad_mesh, "band", -offset))
    grad_nearby = jnp.stack(grad_pieces).reshape(slot_total, mesh_rows, half_width)
    picked = jnp.take(grad_nearby, slot_index, axis=0).astype(fl)
    grad_edge = (0.25 * picked * silu_slope(pre_enc, sig_enc) * live_pairs).astype(bf)
    grad_enc = jnp.einsum("prf,prh->fh", messages, grad_edge, preferred_element_type=fl)
    grad_enc, grad_dec = band_sum([grad_enc, grad_dec])
    return (grid_out, grad_enc, grad_dec)


def solution(mesh):
    placed = (
        P("band", "mp"),
        P("band", None, None, None),
        P("band", "mp"),
        P(None, "mp"),
        P(None, "mp"),
        P("band", "mp"),
        P("band", None),
        P("band"),
    )
    return jax.shard_map(
        local,
        mesh=mesh,
        in_specs=placed,
        out_specs=(P("band", "mp"), P(None, "mp"), P(None, "mp")),
        check_vma=False,
    )
```

```python
import functools

import jax
import jax.numpy as jnp
from jax import lax
from jax.experimental import pallas as pl
from jax.experimental.pallas import tpu as pltpu
from jax.sharding import PartitionSpec as P

REACH = 2
FL, BF = jnp.float32, jnp.bfloat16
ROWS_BY_ROWS = (((0,), (0,)), ((), ()))
COLS_BY_COLS = (((1,), (1,)), ((), ()))


def dot(left, right, dims=(((1,), (0,)), ((), ()))):
    return lax.dot_general(left, right, dims, preferred_element_type=FL)


def swap(value):
    return lax.ppermute(value, "mp", [(0, 1), (1, 0)])


def outward(value, steps):
    count = lax.axis_size("band")
    pairs = []
    for band in range(count):
        pairs.append((2 * band, 2 * ((band + steps) % count)))
        pairs.append((2 * band + 1, 2 * ((band - steps) % count) + 1))
    return lax.ppermute(value, ("band", "mp"), pairs)


def place(pm, block, slot, owner_blocks, facing):
    target = pm[block, slot]
    offset = target // owner_blocks - lax.axis_index("band")
    along = jnp.where(lax.axis_index("mp") == 0, offset, -offset) * facing
    along = jnp.clip(along, -REACH, REACH)
    stored = jnp.where(along >= 0, along, REACH - along)
    return stored * owner_blocks + target % owner_blocks


def live_of(pc, block, slot):
    return jnp.where(slot < pc[block], 1.0, 0.0).astype(FL)


def split_slabs(total, own, mine, other):
    blocks = own.shape[0] // total.shape[1]
    own[...] = total[:blocks].reshape(own.shape).astype(own.dtype)
    mine[...] = total[blocks : 3 * blocks].reshape(mine.shape).astype(mine.dtype)
    other[...] = total[3 * blocks :].reshape(other.shape).astype(other.dtype)


def encode_kernel(pm, pc, a_ref, g_ref, w_ref, x_ref, slope_ref, own, mine, other, total):
    block = pl.program_id(0)
    slots, rows, points = a_ref.shape[1:]
    owner_blocks = own.shape[0] // rows

    @pl.when(block == 0)
    def _():
        total[...] = jnp.zeros_like(total)

    x = dot(a_ref[0].reshape(slots * rows, points), g_ref[...]).astype(BF)
    x_ref[...] = x
    u = dot(x, w_ref[...])
    sig = jax.nn.sigmoid(u)
    edge = u * sig
    slope = sig + edge * (1.0 - sig)
    for slot in range(slots):
        part = slice(slot * rows, (slot + 1) * rows)
        live = live_of(pc, block, slot)
        total[place(pm, block, slot, owner_blocks, 1)] += edge[part] * live
        slope_ref[part] = (slope[part] * (0.25 * live)).astype(BF)

    @pl.when(block == pl.num_programs(0) - 1)
    def _():
        split_slabs(total, own, mine, other)


def gather_near(near, refs, picks):
    blocks = near.shape[0] // len(refs)
    rows, width = near.shape[1], near.shape[2] // 2

    def fill(own_at):
        for at, (ref, pick) in enumerate(zip(refs, picks)):
            for half in range(2):
                column = (own_at + half) % 2 * width
                value = ref[half ^ pick].reshape(blocks, rows, width)
                near[at * blocks : (at + 1) * blocks, :, column : column + width] = value

    core = lax.axis_index("mp")
    pl.when(core == 0)(lambda: fill(0))
    pl.when(core == 1)(lambda: fill(1))


def decode_kernel(
    pm, pc, a_ref, g_ref, cot_ref, w_ref, m, q1, q2, t1, t2,
    out_ref, y_ref, dz_ref, own, mine, other, near, total,
):
    block = pl.program_id(0)
    slots, rows, points = a_ref.shape[1:]
    owner_blocks = own.shape[0] // rows

    @pl.when(block == 0)
    def _():
        total[...] = jnp.zeros_like(total)
        gather_near(near, (m, q1, q2, t1, t2), (0, 0, 0, 1, 1))

    for slot in range(slots):
        chosen = near[place(pm, block, slot, owner_blocks, -1)]
        y = dot(a_ref[0, slot], chosen, ROWS_BY_ROWS).astype(BF)
        y_ref[slot * points : (slot + 1) * points] = y
    z = dot(y_ref[...], w_ref[...])
    sig = jax.nn.sigmoid(z)
    edge = z * sig
    slope = sig + edge * (1.0 - sig)
    result = g_ref[...].astype(FL)
    upstream = cot_ref[...].astype(FL)
    for slot in range(slots):
        part = slice(slot * points, (slot + 1) * points)
        live = live_of(pc, block, slot)
        result = result + edge[part] * live
        dz = ((upstream * live) * slope[part]).astype(BF)
        dz_ref[part] = dz
        total[place(pm, block, slot, owner_blocks, 1)] += dot(a_ref[0, slot], dz)
    out_ref[...] = result.astype(BF)

    @pl.when(block == pl.num_programs(0) - 1)
    def _():
        split_slabs(total, own, mine, other)


def outer_kernel(left_ref, right_ref, out_ref):
    @pl.when(pl.program_id(0) == 0)
    def _():
        out_ref[...] = jnp.zeros_like(out_ref)

    out_ref[...] += dot(left_ref[...], right_ref[...], ROWS_BY_ROWS)


def mesh_grad_kernel(s, t, w_own, w_other, out):
    half = out.shape[2]
    lift_own = (s[0].astype(FL) + t[1].astype(FL)).astype(BF)
    lift_other = (s[1].astype(FL) + t[0].astype(FL)).astype(BF)
    grad = dot(lift_own, w_own[...], COLS_BY_COLS) + dot(lift_other, w_other[...], COLS_BY_COLS)
    grad = grad.astype(BF)
    core = lax.axis_index("mp")

    @pl.when(core == 0)
    def _():
        out[0], out[1] = grad[:, :half], grad[:, half:]

    @pl.when(core == 1)
    def _():
        out[0], out[1] = grad[:, half:], grad[:, :half]


def encoder_grad_kernel(
    pm, pc, x_ref, slope_ref, m, q1, q2, t1, t2, dec_ref, out_ref, near, total
):
    block = pl.program_id(0)
    slots = pm.shape[1]
    rows = near.shape[1]
    owner_blocks = m.shape[1] // rows

    @pl.when(block == 0)
    def _():
        total[...] = jnp.zeros_like(total)
        for at, ref in enumerate((m, q1, q2, t1, t2)):
            near[at * owner_blocks : (at + 1) * owner_blocks] = ref[0].reshape(owner_blocks, rows, -1)

    parts = []
    for slot in range(slots):
        picked = near[place(pm, block, slot, owner_blocks, -1)].astype(FL)
        slope = slope_ref[slot * rows : (slot + 1) * rows].astype(FL)
        parts.append((picked * slope).astype(BF))
    total[...] += dot(x_ref[...], jnp.concatenate(parts, axis=0), ROWS_BY_ROWS)

    @pl.when(block == pl.num_programs(0) - 1)
    def _():
        count, width = total.shape
        for at, value in enumerate((total, dec_ref)):
            for half in range(2):
                start = (2 * at + half) * count
                piece = value[:, half * width // 2 : (half + 1) * width // 2]
                out_ref[start : start + count] = piece.astype(BF)


def sum_kernel(parts_ref, out_ref):
    total = parts_ref[...].astype(FL).sum(axis=0).astype(BF)
    out_ref[...] = jnp.broadcast_to(total[None], out_ref.shape)


def finish_kernel(flat_ref, enc_ref, dec_ref):
    count, width = enc_ref.shape
    for at, out in enumerate((enc_ref, dec_ref)):
        for half in range(2):
            start = (2 * at + half) * count
            out[:, half * width // 2 : (half + 1) * width // 2] = flat_ref[start : start + count].astype(FL)


def params():
    return pltpu.CompilerParams(vmem_limit_bytes=40 * 2**20)


def whole(shape):
    return pl.BlockSpec(shape, lambda *_: (0,) * len(shape))


def shape_of(*shape, dtype=BF):
    return jax.ShapeDtypeStruct(shape, dtype)


def simple(kernel, out_shape):
    return pl.pallas_call(kernel, out_shape=out_shape, compiler_params=params())


def combine(own, parts):
    first, second = (part.astype(FL) for part in parts)
    total = first + second
    return jnp.stack([total[0] + own.astype(FL), total[1]]).astype(BF)


def reduce_to_owner(own, mine, other):
    got = swap(other)
    parts = [outward(jnp.stack([mine[i], got[i]]), i + 1) for i in range(REACH)]
    sums = combine(own, parts)
    return sums, swap(sums)


def spread_from_owner(value):
    near = [outward(value, i + 1) for i in range(REACH)]
    return [value, *near, *(swap(part) for part in near)]


def local(grid, interp, mesh_init, w_enc, w_dec, cotangent, pair_mesh, pair_count):
    blocks, slots, rows, points = interp.shape
    half = grid.shape[1]
    full = w_enc.shape[0]
    owner_rows = mesh_init.shape[0]
    owner_blocks = owner_rows // rows
    near_blocks = (2 * REACH + 1) * owner_blocks
    pairs = blocks * slots

    grid_full = lax.all_gather(grid, "mp", axis=1, tiled=True)
    mesh_both = jnp.stack([mesh_init, swap(mesh_init)])
    w_dec_other = swap(w_dec)

    by_block = lambda *shape: pl.BlockSpec(shape, lambda b, *_: (b,) + (0,) * (len(shape) - 1))
    weights = by_block(1, slots, rows, points)
    slabs = (
        shape_of(owner_rows, half),
        shape_of(REACH, owner_rows, half),
        shape_of(REACH, owner_rows, half),
    )
    slab_specs = [whole(slab.shape) for slab in slabs]
    slab_total = pltpu.VMEM((near_blocks, rows, half), FL)

    x, slope, own, mine, other = pl.pallas_call(
        encode_kernel,
        grid_spec=pltpu.PrefetchScalarGridSpec(
            num_scalar_prefetch=2,
            grid=(blocks,),
            in_specs=[weights, by_block(points, full), whole((full, half))],
            out_specs=[by_block(slots * rows, full), by_block(slots * rows, half), *slab_specs],
            scratch_shapes=[slab_total],
        ),
        out_shape=[shape_of(pairs * rows, full), shape_of(pairs * rows, half), *slabs],
        compiler_params=params(),
    )(pair_mesh, pair_count, interp, grid_full, w_enc)

    sums, got = reduce_to_owner(own, mine, other)
    agg = sums.astype(FL) + got.astype(FL)[::-1]
    mesh_lat = (mesh_both.astype(FL) + 0.25 * agg).astype(BF)
    near = spread_from_owner(mesh_lat)

    out, y, dz, own, mine, other = pl.pallas_call(
        decode_kernel,
        grid_spec=pltpu.PrefetchScalarGridSpec(
            num_scalar_prefetch=2,
            grid=(blocks,),
            in_specs=[
                weights, by_block(points, half), by_block(points, half), whole((full, half)),
                *[whole((2, owner_rows, half))] * 5,
            ],
            out_specs=[
                by_block(points, half), by_block(slots * points, full),
                by_block(slots * points, half), *slab_specs,
            ],
            scratch_shapes=[pltpu.VMEM((near_blocks, rows, full), BF), slab_total],
        ),
        out_shape=[
            shape_of(*grid.shape), shape_of(pairs * points, full),
            shape_of(pairs * points, half), *slabs,
        ],
        compiler_params=params(),
    )(pair_mesh, pair_count, interp, grid, cotangent, w_dec, *near)

    grad_dec = pl.pallas_call(
        outer_kernel,
        grid=(blocks,),
        in_specs=[by_block(slots * points, full), by_block(slots * points, half)],
        out_specs=whole((full, half)),
        out_shape=shape_of(full, half, dtype=FL),
        compiler_params=params(),
        cost_estimate=pl.CostEstimate(
            flops=2 * pairs * points * full * half,
            bytes_accessed=2 * pairs * points * (full + half),
            transcendentals=0,
        ),
    )(y, dz)

    sums, got = reduce_to_owner(own, mine, other)
    grad_mesh = simple(mesh_grad_kernel, shape_of(2, owner_rows, half))(sums, got, w_dec, w_dec_other)
    near = spread_from_owner(grad_mesh)

    pick = lambda at: pl.BlockSpec((1, owner_rows, half), lambda *_: (at, 0, 0))
    flat = pl.pallas_call(
        encoder_grad_kernel,
        grid_spec=pltpu.PrefetchScalarGridSpec(
            num_scalar_prefetch=2,
            grid=(blocks,),
            in_specs=[
                by_block(slots * rows, full), by_block(slots * rows, half),
                pick(0), pick(0), pick(0), pick(1), pick(1), whole((full, half)),
            ],
            out_specs=whole((4 * full, half // 2)),
            scratch_shapes=[pltpu.VMEM((near_blocks, rows, half), BF), pltpu.VMEM((full, half), FL)],
        ),
        out_shape=shape_of(4 * full, half // 2),
        compiler_params=params(),
    )(pair_mesh, pair_count, x, slope, *near, grad_dec)

    count = lax.axis_size("band")
    chunks = lax.all_to_all(flat.reshape(count, -1, half // 2), "band", 0, 0, tiled=True)
    spread = simple(sum_kernel, shape_of(*chunks.shape))(chunks)
    flat = lax.all_to_all(spread, "band", 0, 0, tiled=True).reshape(flat.shape)
    grads = [shape_of(full, half, dtype=FL)] * 2
    grad_enc, grad_dec = simple(finish_kernel, grads)(flat)
    return (out, grad_enc, grad_dec)


def solution(mesh):
    placed = (
        P("band", "mp"),
        P("band", None, None, None),
        P("band", "mp"),
        P(None, "mp"),
        P(None, "mp"),
        P("band", "mp"),
        P("band", None),
        P("band"),
    )
    return jax.shard_map(
        local,
        mesh=mesh,
        in_specs=placed,
        out_specs=(P("band", "mp"), P(None, "mp"), P(None, "mp")),
        check_vma=False,
    )
```

```python
import jax
import jax.numpy as jnp
from jax import lax
from jax.experimental import pallas as pl
from jax.experimental.pallas import tpu as pltpu
from jax.sharding import PartitionSpec as P

REACH = 2
FL, BF = jnp.float32, jnp.bfloat16
ROWS_BY_ROWS = (((0,), (0,)), ((), ()))
COLS_BY_COLS = (((1,), (1,)), ((), ()))


def dot(left, right, dims=(((1,), (0,)), ((), ()))):
    return lax.dot_general(left, right, dims, preferred_element_type=FL)


def swap(value):
    return lax.ppermute(value, "mp", [(0, 1), (1, 0)])


def outward(value, steps):
    count = lax.axis_size("band")
    pairs = []
    for band in range(count - steps):
        pairs.append((2 * band, 2 * (band + steps)))
        pairs.append((2 * (band + steps) + 1, 2 * band + 1))
    return lax.ppermute(value, ("band", "mp"), pairs)


def place(pm, block, slot, owner_blocks, facing):
    target = pm[block, slot]
    offset = target // owner_blocks - lax.axis_index("band")
    along = jnp.where(lax.axis_index("mp") == 0, offset, -offset) * facing
    along = jnp.clip(along, -REACH, REACH)
    stored = jnp.where(along >= 0, along, REACH - along)
    return stored * owner_blocks + target % owner_blocks


def live_of(pc, block, slot):
    return jnp.where(slot < pc[block], 1.0, 0.0).astype(FL)


def split_slabs(total, own, mine, other):
    blocks = own.shape[0] // total.shape[1]
    own[...] = total[:blocks].reshape(own.shape).astype(own.dtype)
    mine[...] = total[blocks : 3 * blocks].reshape(mine.shape).astype(mine.dtype)
    other[...] = total[3 * blocks :].reshape(other.shape).astype(other.dtype)


def encode_kernel(
    pm, pc, a_ref, g_ref, g_other_ref, w_ref, x_ref, slope_ref, own, mine, other, total
):
    block = pl.program_id(0)
    slots, rows, points = a_ref.shape[1:]
    owner_blocks = own.shape[0] // rows

    @pl.when(block == 0)
    def _():
        total[...] = jnp.zeros_like(total)

    first = lax.axis_index("mp") == 0
    g_own, g_other = g_ref[...], g_other_ref[...]
    low, high = jnp.where(first, g_own, g_other), jnp.where(first, g_other, g_own)
    weights = a_ref[0].reshape(slots * rows, points)
    x = dot(weights, jnp.concatenate([low, high], axis=1)).astype(BF)
    x_ref[...] = x
    u = dot(x, w_ref[...])
    sig = jax.nn.sigmoid(u)
    edge = u * sig
    slope = sig + edge * (1.0 - sig)
    for slot in range(slots):
        part = slice(slot * rows, (slot + 1) * rows)
        live = live_of(pc, block, slot)
        total[place(pm, block, slot, owner_blocks, 1)] += edge[part] * live
        slope_ref[part] = (slope[part] * (0.25 * live)).astype(BF)

    @pl.when(block == pl.num_programs(0) - 1)
    def _():
        split_slabs(total, own, mine, other)


def gather_near(near, refs, picks):
    blocks = near.shape[0] // len(refs)
    rows, width = near.shape[1], near.shape[2] // 2

    def fill(own_at):
        for at, (ref, pick) in enumerate(zip(refs, picks)):
            for half in range(2):
                column = (own_at + half) % 2 * width
                value = ref[half ^ pick].reshape(blocks, rows, width)
                near[at * blocks : (at + 1) * blocks, :, column : column + width] = value

    core = lax.axis_index("mp")
    pl.when(core == 0)(lambda: fill(0))
    pl.when(core == 1)(lambda: fill(1))


def decode_kernel(
    pm, pc, a_ref, g_ref, cot_ref, w_ref, m, q1, q2, t1, t2,
    out_ref, y_ref, dz_ref, own, mine, other, near, total,
):
    block = pl.program_id(0)
    slots, rows, points = a_ref.shape[1:]
    owner_blocks = own.shape[0] // rows

    @pl.when(block == 0)
    def _():
        total[...] = jnp.zeros_like(total)
        gather_near(near, (m, q1, q2, t1, t2), (0, 0, 0, 1, 1))

    for slot in range(slots):
        chosen = near[place(pm, block, slot, owner_blocks, -1)]
        y = dot(a_ref[0, slot], chosen, ROWS_BY_ROWS).astype(BF)
        y_ref[slot * points : (slot + 1) * points] = y
    z = dot(y_ref[...], w_ref[...])
    sig = jax.nn.sigmoid(z)
    edge = z * sig
    slope = sig + edge * (1.0 - sig)
    result = g_ref[...].astype(FL)
    upstream = cot_ref[...].astype(FL)
    for slot in range(slots):
        part = slice(slot * points, (slot + 1) * points)
        live = live_of(pc, block, slot)
        result = result + edge[part] * live
        dz = ((upstream * live) * slope[part]).astype(BF)
        dz_ref[part] = dz
        total[place(pm, block, slot, owner_blocks, 1)] += dot(a_ref[0, slot], dz)
    out_ref[...] = result.astype(BF)

    @pl.when(block == pl.num_programs(0) - 1)
    def _():
        split_slabs(total, own, mine, other)


def outer_kernel(left_ref, right_ref, out_ref):
    @pl.when(pl.program_id(0) == 0)
    def _():
        out_ref[...] = jnp.zeros_like(out_ref)

    out_ref[...] += dot(left_ref[...], right_ref[...], ROWS_BY_ROWS)


def mesh_grad_kernel(s, t, w_own, w_other, out):
    half = out.shape[2]
    lift_own = (s[0].astype(FL) + t[1].astype(FL)).astype(BF)
    lift_other = (s[1].astype(FL) + t[0].astype(FL)).astype(BF)
    grad = dot(lift_own, w_own[...], COLS_BY_COLS) + dot(lift_other, w_other[...], COLS_BY_COLS)
    grad = grad.astype(BF)
    core = lax.axis_index("mp")

    @pl.when(core == 0)
    def _():
        out[0], out[1] = grad[:, :half], grad[:, half:]

    @pl.when(core == 1)
    def _():
        out[0], out[1] = grad[:, half:], grad[:, :half]


def encoder_grad_kernel(
    pm, pc, x_ref, slope_ref, m, q1, q2, t1, t2, dec_ref, out_ref, near, total
):
    block = pl.program_id(0)
    slots = pm.shape[1]
    rows = near.shape[1]
    owner_blocks = m.shape[1] // rows

    @pl.when(block == 0)
    def _():
        total[...] = jnp.zeros_like(total)
        for at, ref in enumerate((m, q1, q2, t1, t2)):
            near[at * owner_blocks : (at + 1) * owner_blocks] = ref[0].reshape(owner_blocks, rows, -1)

    parts = []
    for slot in range(slots):
        picked = near[place(pm, block, slot, owner_blocks, -1)].astype(FL)
        slope = slope_ref[slot * rows : (slot + 1) * rows].astype(FL)
        parts.append((picked * slope).astype(BF))
    total[...] += dot(x_ref[...], jnp.concatenate(parts, axis=0), ROWS_BY_ROWS)

    @pl.when(block == pl.num_programs(0) - 1)
    def _():
        count, width = total.shape
        for at, value in enumerate((total, dec_ref)):
            for half in range(2):
                start = (2 * at + half) * count
                piece = value[:, half * width // 2 : (half + 1) * width // 2]
                out_ref[start : start + count] = piece.astype(BF)


def sum_kernel(parts_ref, out_ref):
    total = parts_ref[...].astype(FL).sum(axis=0).astype(BF)
    out_ref[...] = jnp.broadcast_to(total[None], out_ref.shape)


def finish_kernel(flat_ref, enc_ref, dec_ref):
    count, width = enc_ref.shape
    for at, out in enumerate((enc_ref, dec_ref)):
        for half in range(2):
            start = (2 * at + half) * count
            out[:, half * width // 2 : (half + 1) * width // 2] = flat_ref[start : start + count].astype(FL)


def plane_groups(count):
    across = min(16, count // 2)
    plane = [list(range(at, at + across)) for at in range(0, count, across)]
    line = [list(range(at, count, across)) for at in range(across)]
    return plane, line


def exchange(value, groups):
    return lax.all_to_all(value, "band", 0, 0, tiled=True, axis_index_groups=groups)


def params():
    return pltpu.CompilerParams(vmem_limit_bytes=40 * 2**20)


def whole(shape):
    return pl.BlockSpec(shape, lambda *_: (0,) * len(shape))


def shape_of(*shape, dtype=BF):
    return jax.ShapeDtypeStruct(shape, dtype)


def simple(kernel, out_shape):
    return pl.pallas_call(kernel, out_shape=out_shape, compiler_params=params())


def combine(own, parts):
    first, second = (part.astype(FL) for part in parts)
    total = first + second
    return jnp.stack([total[0] + own.astype(FL), total[1]]).astype(BF)


def reduce_to_owner(own, mine, other, beside=None):
    got = swap(other)
    parts = [outward(jnp.stack([mine[i], got[i]]), i + 1) for i in range(REACH)]
    parts, beside = lax.optimization_barrier((parts, beside))
    sums = combine(own, parts)
    return sums, swap(sums), beside


def spread_from_owner(value):
    near = [outward(value, i + 1) for i in range(REACH)]
    return [value, *near, *(swap(part) for part in near)]


def local(grid, interp, mesh_init, w_enc, w_dec, cotangent, pair_mesh, pair_count):
    blocks, slots, rows, points = interp.shape
    half = grid.shape[1]
    full = w_enc.shape[0]
    owner_rows = mesh_init.shape[0]
    owner_blocks = owner_rows // rows
    near_blocks = (2 * REACH + 1) * owner_blocks
    pairs = blocks * slots

    grid_other = swap(grid)
    mesh_both = jnp.stack([mesh_init, swap(mesh_init)])
    w_dec_other = swap(w_dec)

    by_block = lambda *shape: pl.BlockSpec(shape, lambda b, *_: (b,) + (0,) * (len(shape) - 1))
    weights = by_block(1, slots, rows, points)
    slabs = (
        shape_of(owner_rows, half),
        shape_of(REACH, owner_rows, half),
        shape_of(REACH, owner_rows, half),
    )
    slab_specs = [whole(slab.shape) for slab in slabs]
    slab_total = pltpu.VMEM((near_blocks, rows, half), FL)

    x, slope, own, mine, other = pl.pallas_call(
        encode_kernel,
        grid_spec=pltpu.PrefetchScalarGridSpec(
            num_scalar_prefetch=2,
            grid=(blocks,),
            in_specs=[weights, by_block(points, half), by_block(points, half), whole((full, half))],
            out_specs=[by_block(slots * rows, full), by_block(slots * rows, half), *slab_specs],
            scratch_shapes=[slab_total],
        ),
        out_shape=[shape_of(pairs * rows, full), shape_of(pairs * rows, half), *slabs],
        compiler_params=params(),
    )(pair_mesh, pair_count, interp, grid, grid_other, w_enc)

    sums, got, _ = reduce_to_owner(own, mine, other)
    agg = sums.astype(FL) + got.astype(FL)[::-1]
    mesh_lat = (mesh_both.astype(FL) + 0.25 * agg).astype(BF)
    near = spread_from_owner(mesh_lat)

    out, y, dz, own, mine, other = pl.pallas_call(
        decode_kernel,
        grid_spec=pltpu.PrefetchScalarGridSpec(
            num_scalar_prefetch=2,
            grid=(blocks,),
            in_specs=[
                weights, by_block(points, half), by_block(points, half), whole((full, half)),
                *[whole((2, owner_rows, half))] * 5,
            ],
            out_specs=[
                by_block(points, half), by_block(slots * points, full),
                by_block(slots * points, half), *slab_specs,
            ],
            scratch_shapes=[pltpu.VMEM((near_blocks, rows, full), BF), slab_total],
        ),
        out_shape=[
            shape_of(*grid.shape), shape_of(pairs * points, full),
            shape_of(pairs * points, half), *slabs,
        ],
        compiler_params=params(),
    )(pair_mesh, pair_count, interp, grid, cotangent, w_dec, *near)

    grad_dec = pl.pallas_call(
        outer_kernel,
        grid=(blocks,),
        in_specs=[by_block(slots * points, full), by_block(slots * points, half)],
        out_specs=whole((full, half)),
        out_shape=shape_of(full, half, dtype=FL),
        compiler_params=params(),
        cost_estimate=pl.CostEstimate(
            flops=2 * pairs * points * full * half,
            bytes_accessed=2 * pairs * points * (full + half),
            transcendentals=0,
        ),
    )(y, dz)

    sums, got, grad_dec = reduce_to_owner(own, mine, other, grad_dec)
    grad_mesh = simple(mesh_grad_kernel, shape_of(2, owner_rows, half))(sums, got, w_dec, w_dec_other)
    near = spread_from_owner(grad_mesh)

    pick = lambda at: pl.BlockSpec((1, owner_rows, half), lambda *_: (at, 0, 0))
    flat = pl.pallas_call(
        encoder_grad_kernel,
        grid_spec=pltpu.PrefetchScalarGridSpec(
            num_scalar_prefetch=2,
            grid=(blocks,),
            in_specs=[
                by_block(slots * rows, full), by_block(slots * rows, half),
                pick(0), pick(0), pick(0), pick(1), pick(1), whole((full, half)),
            ],
            out_specs=whole((4 * full, half // 2)),
            scratch_shapes=[pltpu.VMEM((near_blocks, rows, half), BF), pltpu.VMEM((full, half), FL)],
        ),
        out_shape=shape_of(4 * full, half // 2),
        compiler_params=params(),
    )(pair_mesh, pair_count, x, slope, *near, grad_dec)

    plane, line = plane_groups(lax.axis_size("band"))
    across = len(plane[0])
    chunks = exchange(flat.reshape(across, -1, half // 2), plane)
    piece = simple(sum_kernel, shape_of(len(line[0]), *chunks.shape[1:]))(chunks)
    pieces = exchange(piece, line)
    spread = simple(sum_kernel, shape_of(*chunks.shape))(pieces)
    flat = exchange(spread, plane).reshape(flat.shape)
    grads = [shape_of(full, half, dtype=FL)] * 2
    grad_enc, grad_dec = simple(finish_kernel, grads)(flat)
    return (out, grad_enc, grad_dec)


def solution(mesh):
    placed = (
        P("band", "mp"),
        P("band", None, None, None),
        P("band", "mp"),
        P(None, "mp"),
        P(None, "mp"),
        P("band", "mp"),
        P("band", None),
        P("band"),
    )
    return jax.shard_map(
        local,
        mesh=mesh,
        in_specs=placed,
        out_specs=(P("band", "mp"), P(None, "mp"), P(None, "mp")),
        check_vma=False,
    )
```

```python
import jax
import jax.numpy as jnp
from jax import lax
from jax.experimental import pallas as pl
from jax.experimental.pallas import tpu as pltpu
from jax.sharding import PartitionSpec as P

REACH = 2
NEAR = 2 * REACH + 1
OWNER_BLOCKS = 2

FL, BF = jnp.float32, jnp.bfloat16
ROWS_BY_ROWS = (((0,), (0,)), ((), ()))
COLS_BY_COLS = (((1,), (1,)), ((), ()))


def dot(left, right, dims=(((1,), (0,)), ((), ()))):
    return lax.dot_general(left, right, dims, preferred_element_type=FL)


def swap(value):
    return lax.ppermute(value, "mp", [(0, 1), (1, 0)])


def outward(value, steps):
    count = lax.axis_size("band")
    pairs = []
    for band in range(count - steps):
        pairs.append((2 * band, 2 * (band + steps)))
        pairs.append((2 * (band + steps) + 1, 2 * band + 1))
    return lax.ppermute(value, ("band", "mp"), pairs)


def place(pm, block, slot, facing):
    target = pm[slot, block]
    offset = target // OWNER_BLOCKS - lax.axis_index("band")
    along = jnp.where(lax.axis_index("mp") == 0, offset, -offset) * facing
    along = jnp.clip(along, -REACH, REACH)
    stored = jnp.where(along >= 0, along, REACH - along)
    return stored * OWNER_BLOCKS + target % OWNER_BLOCKS


def live_of(pc, block, slot):
    return jnp.where(slot < pc[block], 1.0, 0.0).astype(FL)


def split_slabs(total, own, mine, other):
    blocks = own.shape[0] // total.shape[1]
    own[...] = total[:blocks].reshape(own.shape).astype(own.dtype)
    mine[...] = total[blocks : 3 * blocks].reshape(mine.shape).astype(mine.dtype)
    other[...] = total[3 * blocks :].reshape(other.shape).astype(other.dtype)


def sigmoid(value):
    return 0.5 * jnp.tanh(0.5 * value) + 0.5


def fetch(pairs, sems):
    copies = [pltpu.make_async_copy(src, dst, sems.at[at]) for at, (src, dst) in enumerate(pairs)]
    for copy in copies:
        copy.start()
    return copies


def encode_kernel(
    pm, pc, a_hbm, g_hbm, w_hbm, g_other, a_ref, x_ref, slope_ref, own, mine, other,
    total, g_ref, w_ref, sems,
):
    blocks, slots, rows, points = a_ref.shape
    pairs = slots * rows
    early = min(2, blocks)
    head, tail = pl.ds(0, early), pl.ds(early, blocks - early)
    copies = fetch(
        [(g_hbm, g_ref), (a_hbm.at[head], a_ref.at[head]), (w_hbm, w_ref), (a_hbm.at[tail], a_ref.at[tail])],
        sems,
    )
    total[...] = jnp.zeros_like(total)
    first = lax.axis_index("mp") == 0
    for copy in copies[:3]:
        copy.wait()
    for block in range(blocks):
        if block == early:
            copies[3].wait()
        span = slice(block * points, (block + 1) * points)
        g_own, g_far = g_ref[span], g_other[span]
        low, high = jnp.where(first, g_own, g_far), jnp.where(first, g_far, g_own)
        weights = a_ref[block].reshape(pairs, points)
        x = dot(weights, jnp.concatenate([low, high], axis=1)).astype(BF)
        x_ref[block * pairs : (block + 1) * pairs] = x
        u = dot(x, w_ref[...])
        for slot in range(slots):
            part = u[slot * rows : (slot + 1) * rows]
            sig = sigmoid(part)
            edge = part * sig
            live = live_of(pc, block, slot)
            total[place(pm, block, slot, 1)] += edge * live
            slope = (sig + edge * (1.0 - sig)) * (0.25 * live)
            slope_ref[block * pairs + slot * rows : block * pairs + (slot + 1) * rows] = slope.astype(BF)
    split_slabs(total, own, mine, other)


def gather_near(near, refs, picks):
    blocks = near.shape[0] // len(refs)
    rows, width = near.shape[1], near.shape[2] // 2

    def fill(own_at):
        for at, (ref, pick) in enumerate(zip(refs, picks)):
            for half in range(2):
                column = (own_at + half) % 2 * width
                value = ref[half ^ pick].reshape(blocks, rows, width)
                near[at * blocks : (at + 1) * blocks, :, column : column + width] = value

    core = lax.axis_index("mp")
    pl.when(core == 0)(lambda: fill(0))
    pl.when(core == 1)(lambda: fill(1))


def decode_kernel(
    pm, pc, a_ref, g_ref, cot_ref, w_ref, m, q1, q2, t1, t2,
    out_ref, y_ref, dz_ref, own, mine, other, near, total,
):
    blocks, slots, rows, points = a_ref.shape
    pairs = slots * points
    total[...] = jnp.zeros_like(total)
    gather_near(near, (m, q1, q2, t1, t2), (0, 0, 0, 1, 1))
    for block in range(blocks):
        for slot in range(slots):
            chosen = near[place(pm, block, slot, -1)]
            y = dot(a_ref[block, slot], chosen, ROWS_BY_ROWS).astype(BF)
            y_ref[block * pairs + slot * points : block * pairs + (slot + 1) * points] = y
        span = slice(block * points, (block + 1) * points)
        z = dot(y_ref[block * pairs : (block + 1) * pairs], w_ref[...])
        result = g_ref[span].astype(FL)
        upstream = cot_ref[span].astype(FL)
        for slot in range(slots):
            part = z[slot * points : (slot + 1) * points]
            sig = sigmoid(part)
            edge = part * sig
            live = live_of(pc, block, slot)
            result = result + edge * live
            slope = sig + edge * (1.0 - sig)
            dz = ((upstream * live) * slope).astype(BF)
            dz_ref[block * pairs + slot * points : block * pairs + (slot + 1) * points] = dz
            total[place(pm, block, slot, 1)] += dot(a_ref[block, slot], dz)
        out_ref[span] = result.astype(BF)
    split_slabs(total, own, mine, other)


def outer_kernel(left_ref, right_ref, out_ref):
    out_ref[...] = dot(right_ref[...], left_ref[...], ROWS_BY_ROWS)


def mesh_grad_kernel(s, t, w_own, w_other, out):
    half = out.shape[2]
    lift_own = (s[0].astype(FL) + t[1].astype(FL)).astype(BF)
    lift_other = (s[1].astype(FL) + t[0].astype(FL)).astype(BF)
    grad = dot(lift_own, w_own[...], COLS_BY_COLS) + dot(lift_other, w_other[...], COLS_BY_COLS)
    grad = grad.astype(BF)
    core = lax.axis_index("mp")

    @pl.when(core == 0)
    def _():
        out[0], out[1] = grad[:, :half], grad[:, half:]

    @pl.when(core == 1)
    def _():
        out[0], out[1] = grad[:, half:], grad[:, :half]


def encoder_grad_kernel(
    pm, pc, x_ref, slope_ref, m, q1, q2, t1, t2, dec_ref, out_ref, near, total
):
    slots, blocks = pm.shape
    rows = near.shape[1]
    pairs = slots * rows
    for at, ref in enumerate((m, q1, q2, t1, t2)):
        near[at * OWNER_BLOCKS : (at + 1) * OWNER_BLOCKS] = ref[at // 3].reshape(OWNER_BLOCKS, rows, -1)
    for block in range(blocks):
        parts = []
        for slot in range(slots):
            picked = near[place(pm, block, slot, -1)].astype(FL)
            start = block * pairs + slot * rows
            parts.append((picked * slope_ref[start : start + rows].astype(FL)).astype(BF))
        term = dot(jnp.concatenate(parts, axis=0), x_ref[block * pairs : (block + 1) * pairs], ROWS_BY_ROWS)
        total[...] = term if block == 0 else total[...] + term
    count, width = total.shape
    lanes = out_ref.shape[1]
    for at, value in enumerate((total, dec_ref)):
        for tile in range(width // lanes):
            start = (at * width // lanes + tile) * count
            out_ref[start : start + count] = value[:, tile * lanes : (tile + 1) * lanes].astype(BF)


def sum_kernel(parts_ref, out_ref):
    total = parts_ref[...].astype(FL).sum(axis=0).astype(BF)
    out_ref[...] = jnp.broadcast_to(total[None], out_ref.shape)


def finish_kernel(flat_ref, enc_ref, dec_ref):
    lanes = flat_ref.shape[1]
    width, count = enc_ref.shape
    for at, out in enumerate((enc_ref, dec_ref)):
        for tile in range(width // lanes):
            start = (at * width // lanes + tile) * count
            piece = flat_ref[start : start + count].astype(FL)
            out[tile * lanes : (tile + 1) * lanes] = piece.T


def plane_groups(count):
    across = min(16, count // 2)
    plane = [list(range(at, at + across)) for at in range(0, count, across)]
    line = [list(range(at, count, across)) for at in range(across)]
    return plane, line


def exchange(value, groups):
    return lax.all_to_all(value, "band", 0, 0, tiled=True, axis_index_groups=groups)


def params():
    return pltpu.CompilerParams(vmem_limit_bytes=40 * 2**20)


def shape_of(*shape, dtype=BF):
    return jax.ShapeDtypeStruct(shape, dtype)


def simple(kernel, out_shape):
    return pl.pallas_call(kernel, out_shape=out_shape, compiler_params=params())


def combine(own, parts):
    first, second = (part.astype(FL) for part in parts)
    total = first + second
    return jnp.stack([total[0] + own.astype(FL), total[1]]).astype(BF)


def reduce_to_owner(own, mine, other, beside=None):
    got = swap(other)
    parts = [outward(jnp.stack([mine[i], got[i]]), i + 1) for i in range(REACH)]
    parts, beside = lax.optimization_barrier((parts, beside))
    sums = combine(own, parts)
    return sums, swap(sums), beside


def spread_from_owner(value):
    near = [outward(value, i + 1) for i in range(REACH)]
    return [value, *near, *(swap(part) for part in near)]


VMEM, ANY, SMEM = (pl.BlockSpec(memory_space=space) for space in (pltpu.VMEM, pl.ANY, pltpu.SMEM))


def held(kernel, in_specs, out_shape, scratch=(), cost=None):
    return pl.pallas_call(
        kernel,
        in_specs=in_specs,
        out_specs=jax.tree.map(lambda _: VMEM, out_shape),
        out_shape=out_shape,
        scratch_shapes=scratch,
        compiler_params=params(),
        cost_estimate=cost,
    )


def slab_shapes(owner_rows, half):
    return [shape_of(*lead, owner_rows, half) for lead in ((), (REACH,), (REACH,))]


def encode(pair_mesh, pair_count, interp, grid, grid_other, w_enc):
    blocks, slots, rows, points = interp.shape
    full, half = w_enc.shape
    pairs = blocks * slots * rows
    return held(
        encode_kernel,
        [SMEM, SMEM, ANY, ANY, ANY, VMEM],
        [
            shape_of(*interp.shape), shape_of(pairs, full), shape_of(pairs, half),
            *slab_shapes(OWNER_BLOCKS * rows, half),
        ],
        [
            pltpu.VMEM((NEAR * OWNER_BLOCKS, rows, half), FL), pltpu.VMEM(grid.shape, BF),
            pltpu.VMEM(w_enc.shape, BF), pltpu.SemaphoreType.DMA((4,)),
        ],
    )(pair_mesh, pair_count, interp, grid, w_enc, grid_other)


def decode(pair_mesh, pair_count, interp, grid, cotangent, w_dec, near):
    blocks, slots, rows, points = interp.shape
    full, half = w_dec.shape
    pairs = blocks * slots * points
    return held(
        decode_kernel,
        [SMEM, SMEM, *[VMEM] * (4 + NEAR)],
        [
            shape_of(*grid.shape), shape_of(pairs, full), shape_of(pairs, half),
            *slab_shapes(OWNER_BLOCKS * rows, half),
        ],
        [
            pltpu.VMEM((NEAR * OWNER_BLOCKS, rows, full), BF),
            pltpu.VMEM((NEAR * OWNER_BLOCKS, rows, half), FL),
        ],
    )(pair_mesh, pair_count, interp, grid, cotangent, w_dec, *near)


def outer(y, dz):
    pairs, full = y.shape
    half = dz.shape[1]
    cost = pl.CostEstimate(
        flops=2 * pairs * full * half, bytes_accessed=2 * pairs * (full + half), transcendentals=0
    )
    return held(outer_kernel, [VMEM, VMEM], shape_of(half, full, dtype=FL), cost=cost)(y, dz)


def encoder_grad(pair_mesh, pair_count, x, slope, near, grad_dec):
    full, half = x.shape[1], slope.shape[1]
    rows = near[0].shape[1] // OWNER_BLOCKS
    return held(
        encoder_grad_kernel,
        [SMEM, SMEM, *[VMEM] * (3 + NEAR)],
        shape_of(4 * full, half // 2),
        [pltpu.VMEM((NEAR * OWNER_BLOCKS, rows, half), BF), pltpu.VMEM((half, full), FL)],
    )(pair_mesh, pair_count, x, slope, *near, grad_dec)


def local(grid, interp, mesh_init, w_enc, w_dec, cotangent, pair_mesh, pair_count):
    full, half = w_enc.shape
    pair_mesh = pair_mesh.T
    grid_other = swap(grid)
    mesh_both = jnp.stack([mesh_init, swap(mesh_init)])
    w_dec_other = swap(w_dec)

    interp, x, slope, own, mine, other = encode(pair_mesh, pair_count, interp, grid, grid_other, w_enc)
    sums, got, _ = reduce_to_owner(own, mine, other)
    agg = sums.astype(FL) + got.astype(FL)[::-1]
    mesh_lat = (mesh_both.astype(FL) + 0.25 * agg).astype(BF)
    near = spread_from_owner(mesh_lat)

    out, y, dz, own, mine, other = decode(
        pair_mesh, pair_count, interp, grid, cotangent, w_dec, near
    )
    sums, got, grad_dec = reduce_to_owner(own, mine, other, outer(y, dz))
    grad_mesh = simple(mesh_grad_kernel, shape_of(*sums.shape))(sums, got, w_dec, w_dec_other)
    near = spread_from_owner(grad_mesh)
    flat = encoder_grad(pair_mesh, pair_count, x, slope, near, grad_dec)

    plane, line = plane_groups(lax.axis_size("band"))
    across = len(plane[0])
    chunks = exchange(flat.reshape(across, -1, half // 2), plane)
    piece = simple(sum_kernel, shape_of(len(line[0]), *chunks.shape[1:]))(chunks)
    pieces = exchange(piece, line)
    spread = simple(sum_kernel, shape_of(*chunks.shape))(pieces)
    flat = exchange(spread, plane).reshape(flat.shape)
    grads = [shape_of(full, half, dtype=FL)] * 2
    grad_enc, grad_dec = simple(finish_kernel, grads)(flat)
    return (out, grad_enc, grad_dec)


def solution(mesh):
    placed = (
        P("band", "mp"),
        P("band", None, None, None),
        P("band", "mp"),
        P(None, "mp"),
        P(None, "mp"),
        P("band", "mp"),
        P("band", None),
        P("band"),
    )
    return jax.shard_map(
        local,
        mesh=mesh,
        in_specs=placed,
        out_specs=(P("band", "mp"), P(None, "mp"), P(None, "mp")),
        check_vma=False,
    )
```

```python
import jax
import jax.numpy as jnp
from jax import lax
from jax.experimental import pallas as pl
from jax.experimental.pallas import tpu as pltpu
from jax.sharding import PartitionSpec as P

REACH = 2
NEAR = 2 * REACH + 1
OWNER_BLOCKS = 2

FL, BF = jnp.float32, jnp.bfloat16
ROWS_BY_ROWS = (((0,), (0,)), ((), ()))
COLS_BY_COLS = (((1,), (1,)), ((), ()))


def dot(left, right, dims=(((1,), (0,)), ((), ()))):
    return lax.dot_general(left, right, dims, preferred_element_type=FL)


def swap(value):
    return lax.ppermute(value, "mp", [(0, 1), (1, 0)])


def outward(value, steps):
    count = lax.axis_size("band")
    pairs = []
    for band in range(count - steps):
        pairs.append((2 * band, 2 * (band + steps)))
        pairs.append((2 * (band + steps) + 1, 2 * band + 1))
    return lax.ppermute(value, ("band", "mp"), pairs)


def place(pm, block, slot, facing):
    target = pm[slot, block]
    offset = target // OWNER_BLOCKS - lax.axis_index("band")
    along = jnp.where(lax.axis_index("mp") == 0, offset, -offset) * facing
    along = jnp.clip(along, -REACH, REACH)
    stored = jnp.where(along >= 0, along, REACH - along)
    return stored * OWNER_BLOCKS + target % OWNER_BLOCKS


def live_of(pc, block, slot):
    return jnp.where(slot < pc[block], 1.0, 0.0).astype(FL)


def split_slabs(total, own, mine, other):
    blocks = own.shape[0] // total.shape[1]
    own[...] = total[:blocks].reshape(own.shape).astype(own.dtype)
    mine[...] = total[blocks : 3 * blocks].reshape(mine.shape).astype(mine.dtype)
    other[...] = total[3 * blocks :].reshape(other.shape).astype(other.dtype)


def sigmoid(value):
    return 0.5 * jnp.tanh(0.5 * value) + 0.5


def fetch(pairs, sems):
    copies = [pltpu.make_async_copy(src, dst, sems.at[at]) for at, (src, dst) in enumerate(pairs)]
    for copy in copies:
        copy.start()
    return copies


def lift_kernel(a_hbm, g_hbm, w_hbm, pm_hbm, pc_hbm, a_ref, w_ref, x_ref, pm_ref, pc_ref, g_ref, sems):
    blocks, slots, rows, points = a_ref.shape
    pairs = slots * rows
    early = min(3, blocks)
    head, tail = pl.ds(0, early), pl.ds(early, blocks - early)
    copies = fetch(
        [
            (g_hbm, g_ref), (a_hbm.at[head], a_ref.at[head]), (a_hbm.at[tail], a_ref.at[tail]),
            (w_hbm, w_ref), (pm_hbm, pm_ref), (pc_hbm, pc_ref),
        ],
        sems,
    )
    for copy in copies[:2]:
        copy.wait()
    for block in range(blocks):
        if block == early:
            copies[2].wait()
        weights = a_ref[block].reshape(pairs, points)
        x = dot(weights, g_ref[block * points : (block + 1) * points])
        x_ref[block * pairs : (block + 1) * pairs] = x.astype(BF)
    for copy in copies[3:]:
        copy.wait()


def encode_kernel(
    pm, pc, a_ref, w_ref, x_own, g_other, x_other, slope_ref, own, mine, other, total
):
    blocks, slots, rows, points = a_ref.shape
    pairs = slots * rows
    half = x_own.shape[1]
    core = lax.axis_index("mp")
    w_own = w_ref[pl.ds(pl.multiple_of(core * half, half), half)]
    w_far = w_ref[pl.ds(pl.multiple_of((1 - core) * half, half), half)]
    total[...] = jnp.zeros_like(total)
    for block in range(blocks):
        span = slice(block * pairs, (block + 1) * pairs)
        weights = a_ref[block].reshape(pairs, points)
        x = dot(weights, g_other[block * points : (block + 1) * points]).astype(BF)
        x_other[span] = x
        u = dot(x_own[span], w_own) + dot(x, w_far)
        for slot in range(slots):
            part = u[slot * rows : (slot + 1) * rows]
            sig = sigmoid(part)
            edge = part * sig
            live = live_of(pc, block, slot)
            total[place(pm, block, slot, 1)] += edge * live
            slope = (sig + edge * (1.0 - sig)) * (0.25 * live)
            slope_ref[block * pairs + slot * rows : block * pairs + (slot + 1) * rows] = slope.astype(BF)
    split_slabs(total, own, mine, other)


def gather_near(near, refs, picks):
    blocks = near.shape[0] // len(refs)
    rows, width = near.shape[1], near.shape[2] // 2

    def fill(own_at):
        for at, (ref, pick) in enumerate(zip(refs, picks)):
            for half in range(2):
                column = (own_at + half) % 2 * width
                value = ref[half ^ pick].reshape(blocks, rows, width)
                near[at * blocks : (at + 1) * blocks, :, column : column + width] = value

    core = lax.axis_index("mp")
    pl.when(core == 0)(lambda: fill(0))
    pl.when(core == 1)(lambda: fill(1))


def decode_kernel(
    pm, pc, a_ref, g_ref, cot_ref, w_ref, m, q1, q2, t1, t2,
    out_ref, y_ref, dz_ref, own, mine, other, near, total,
):
    blocks, slots, rows, points = a_ref.shape
    pairs = slots * points
    total[...] = jnp.zeros_like(total)
    gather_near(near, (m, q1, q2, t1, t2), (0, 0, 0, 1, 1))
    for block in range(blocks):
        for slot in range(slots):
            chosen = near[place(pm, block, slot, -1)]
            y = dot(a_ref[block, slot], chosen, ROWS_BY_ROWS).astype(BF)
            y_ref[block * pairs + slot * points : block * pairs + (slot + 1) * points] = y
        span = slice(block * points, (block + 1) * points)
        z = dot(y_ref[block * pairs : (block + 1) * pairs], w_ref[...])
        result = g_ref[span].astype(FL)
        upstream = cot_ref[span].astype(FL)
        for slot in range(slots):
            part = z[slot * points : (slot + 1) * points]
            sig = sigmoid(part)
            edge = part * sig
            live = live_of(pc, block, slot)
            result = result + edge * live
            slope = sig + edge * (1.0 - sig)
            dz = ((upstream * live) * slope).astype(BF)
            dz_ref[block * pairs + slot * points : block * pairs + (slot + 1) * points] = dz
            total[place(pm, block, slot, 1)] += dot(a_ref[block, slot], dz)
        out_ref[span] = result.astype(BF)
    split_slabs(total, own, mine, other)


def outer_kernel(left_ref, right_ref, made_ref, out_ref, sent_ref):
    out_ref[...] = dot(right_ref[...], left_ref[...], ROWS_BY_ROWS)
    sent_ref[...] = made_ref[...]


def mesh_grad_kernel(s, t, w_own, w_other, out):
    half = out.shape[2]
    lift_own = (s[0].astype(FL) + t[1].astype(FL)).astype(BF)
    lift_other = (s[1].astype(FL) + t[0].astype(FL)).astype(BF)
    grad = dot(lift_own, w_own[...], COLS_BY_COLS) + dot(lift_other, w_other[...], COLS_BY_COLS)
    grad = grad.astype(BF)
    core = lax.axis_index("mp")

    @pl.when(core == 0)
    def _():
        out[0], out[1] = grad[:, :half], grad[:, half:]

    @pl.when(core == 1)
    def _():
        out[0], out[1] = grad[:, half:], grad[:, :half]


def encoder_grad_kernel(
    pm, pc, x_own, x_other, slope_ref, m, q1, q2, t1, t2, dec_ref, out_ref, near, total
):
    slots, blocks = pm.shape
    rows = near.shape[1]
    pairs = slots * rows
    for at, ref in enumerate((m, q1, q2, t1, t2)):
        near[at * OWNER_BLOCKS : (at + 1) * OWNER_BLOCKS] = ref[at // 3].reshape(OWNER_BLOCKS, rows, -1)
    for block in range(blocks):
        parts = []
        for slot in range(slots):
            picked = near[place(pm, block, slot, -1)].astype(FL)
            start = block * pairs + slot * rows
            parts.append((picked * slope_ref[start : start + rows].astype(FL)).astype(BF))
        du = jnp.concatenate(parts, axis=0)
        for at, x_ref in enumerate((x_own, x_other)):
            term = dot(du, x_ref[block * pairs : (block + 1) * pairs], ROWS_BY_ROWS)
            total[at] = term if block == 0 else total[at] + term
    count, half = total.shape[1:]
    lanes = out_ref.shape[1]
    tiles = half // lanes

    def store(tile, value):
        out_ref[tile * count : (tile + 1) * count] = value.astype(BF)

    def store_encoder(order):
        for at, side in enumerate(order):
            for tile in range(tiles):
                store(at * tiles + tile, total[side, :, tile * lanes : (tile + 1) * lanes])

    core = lax.axis_index("mp")
    pl.when(core == 0)(lambda: store_encoder((0, 1)))
    pl.when(core == 1)(lambda: store_encoder((1, 0)))
    for tile in range(2 * tiles):
        store(2 * tiles + tile, dec_ref[:, tile * lanes : (tile + 1) * lanes])


def sum_kernel(parts_ref, out_ref):
    total = parts_ref[...].astype(FL).sum(axis=0).astype(BF)
    out_ref[...] = jnp.broadcast_to(total[None], out_ref.shape)


def finish_kernel(flat_ref, enc_ref, dec_ref):
    lanes = flat_ref.shape[1]
    width, count = enc_ref.shape
    for at, out in enumerate((enc_ref, dec_ref)):
        for tile in range(width // lanes):
            start = (at * width // lanes + tile) * count
            piece = flat_ref[start : start + count].astype(FL)
            out[tile * lanes : (tile + 1) * lanes] = piece.T


def plane_groups(count):
    across = min(16, count // 2)
    plane = [list(range(at, at + across)) for at in range(0, count, across)]
    line = [list(range(at, count, across)) for at in range(across)]
    return plane, line


def exchange(value, groups):
    return lax.all_to_all(value, "band", 0, 0, tiled=True, axis_index_groups=groups)


def params():
    return pltpu.CompilerParams(vmem_limit_bytes=24 * 2**20)


def shape_of(*shape, dtype=BF):
    return jax.ShapeDtypeStruct(shape, dtype)


def simple(kernel, out_shape):
    return pl.pallas_call(kernel, out_shape=out_shape, compiler_params=params())


def combine(own, parts):
    first, second = (part.astype(FL) for part in parts)
    total = first + second
    return jnp.stack([total[0] + own.astype(FL), total[1]]).astype(BF)


def reduce_to_owner(own, mine, other, beside=None):
    got = swap(other)
    parts = [outward(jnp.stack([mine[i], got[i]]), i + 1) for i in range(REACH)]
    parts, beside = lax.optimization_barrier((parts, beside))
    sums = combine(own, parts)
    return sums, swap(sums), beside


def spread_from_owner(value):
    near = [outward(value, i + 1) for i in range(REACH)]
    return [value, *near, *(swap(part) for part in near)]


VMEM, HBM, SMEM = (pl.BlockSpec(memory_space=space) for space in (pltpu.VMEM, pltpu.HBM, pltpu.SMEM))


def held(kernel, in_specs, out_shape, scratch=(), cost=None):
    return pl.pallas_call(
        kernel,
        in_specs=in_specs,
        out_specs=jax.tree.map(lambda _: VMEM, out_shape),
        out_shape=out_shape,
        scratch_shapes=scratch,
        compiler_params=params(),
        cost_estimate=cost,
    )


def slab_shapes(owner_rows, half):
    return [shape_of(*lead, owner_rows, half) for lead in ((), (REACH,), (REACH,))]


def lift_own(*given):
    interp, grid, w_enc, pair_mesh, pair_count = given
    blocks, slots, rows, points = interp.shape
    half = w_enc.shape[1]
    pairs = blocks * slots * rows
    cost = pl.CostEstimate(flops=2 * pairs * points * half, bytes_accessed=4 * 2**20, transcendentals=0)
    fixed = [jax.ShapeDtypeStruct(value.shape, value.dtype) for value in (pair_mesh, pair_count)]
    return pl.pallas_call(
        lift_kernel,
        in_specs=[HBM] * 5,
        out_specs=[VMEM, VMEM, VMEM, SMEM, SMEM],
        out_shape=[shape_of(*interp.shape), shape_of(*w_enc.shape), shape_of(pairs, half), *fixed],
        scratch_shapes=[pltpu.VMEM(grid.shape, BF), pltpu.SemaphoreType.DMA((6,))],
        compiler_params=params(),
        cost_estimate=cost,
    )(*(pltpu.with_memory_space_constraint(value, pltpu.HBM) for value in given))


def encode(pair_mesh, pair_count, interp, w_enc, x_own, grid_other):
    blocks, slots, rows, points = interp.shape
    pairs, half = x_own.shape
    return held(
        encode_kernel,
        [SMEM, SMEM, *[VMEM] * 4],
        [shape_of(pairs, half), shape_of(pairs, half), *slab_shapes(OWNER_BLOCKS * rows, half)],
        [pltpu.VMEM((NEAR * OWNER_BLOCKS, rows, half), FL)],
    )(pair_mesh, pair_count, interp, w_enc, x_own, grid_other)


def decode(pair_mesh, pair_count, interp, grid, cotangent, w_dec, near):
    blocks, slots, rows, points = interp.shape
    full, half = w_dec.shape
    pairs = blocks * slots * points
    return held(
        decode_kernel,
        [SMEM, SMEM, *[VMEM] * (4 + NEAR)],
        [
            shape_of(*grid.shape), shape_of(pairs, full), shape_of(pairs, half),
            *slab_shapes(OWNER_BLOCKS * rows, half),
        ],
        [
            pltpu.VMEM((NEAR * OWNER_BLOCKS, rows, full), BF),
            pltpu.VMEM((NEAR * OWNER_BLOCKS, rows, half), FL),
        ],
    )(pair_mesh, pair_count, interp, grid, cotangent, w_dec, *near)


def outer(y, dz, made):
    pairs, full = y.shape
    half = dz.shape[1]
    cost = pl.CostEstimate(
        flops=2 * pairs * full * half, bytes_accessed=2 * pairs * (full + half), transcendentals=0
    )
    outs = [shape_of(half, full, dtype=FL), shape_of(*made.shape)]
    return held(outer_kernel, [VMEM] * 3, outs, cost=cost)(y, dz, made)


def encoder_grad(pair_mesh, pair_count, x_own, x_other, slope, near, grad_dec):
    half = slope.shape[1]
    rows = near[0].shape[1] // OWNER_BLOCKS
    return held(
        encoder_grad_kernel,
        [SMEM, SMEM, *[VMEM] * (4 + NEAR)],
        shape_of(8 * half, half // 2),
        [pltpu.VMEM((NEAR * OWNER_BLOCKS, rows, half), BF), pltpu.VMEM((2, half, half), FL)],
    )(pair_mesh, pair_count, x_own, x_other, slope, *near, grad_dec)


def local(grid, interp, mesh_init, w_enc, w_dec, cotangent, pair_mesh, pair_count):
    full, half = w_enc.shape
    pair_mesh = pair_mesh.T
    grid_other = swap(grid)
    mesh_both = jnp.stack([mesh_init, swap(mesh_init)])
    w_dec_other = swap(w_dec)

    interp, w_enc, x_own, pair_mesh, pair_count = lift_own(interp, grid, w_enc, pair_mesh, pair_count)
    x_other, slope, own, mine, other = encode(
        pair_mesh, pair_count, interp, w_enc, x_own, grid_other
    )
    sums, got, _ = reduce_to_owner(own, mine, other)
    agg = sums.astype(FL) + got.astype(FL)[::-1]
    mesh_lat = (mesh_both.astype(FL) + 0.25 * agg).astype(BF)
    near = spread_from_owner(mesh_lat)

    out, y, dz, own, mine, other = decode(
        pair_mesh, pair_count, interp, grid, cotangent, w_dec, near
    )
    sums, got, (grad_dec, out) = reduce_to_owner(own, mine, other, outer(y, dz, out))
    grad_mesh = simple(mesh_grad_kernel, shape_of(*sums.shape))(sums, got, w_dec, w_dec_other)
    near = spread_from_owner(grad_mesh)
    flat = encoder_grad(pair_mesh, pair_count, x_own, x_other, slope, near, grad_dec)

    plane, line = plane_groups(lax.axis_size("band"))
    across = len(plane[0])
    chunks = exchange(flat.reshape(across, -1, half // 2), plane)
    piece = simple(sum_kernel, shape_of(len(line[0]), *chunks.shape[1:]))(chunks)
    pieces = exchange(piece, line)
    spread = simple(sum_kernel, shape_of(*chunks.shape))(pieces)
    flat = exchange(spread, plane).reshape(flat.shape)
    grads = [shape_of(full, half, dtype=FL)] * 2
    grad_enc, grad_dec = simple(finish_kernel, grads)(flat)
    return (out, grad_enc, grad_dec)


def solution(mesh):
    placed = (
        P("band", "mp"),
        P("band", None, None, None),
        P("band", "mp"),
        P(None, "mp"),
        P(None, "mp"),
        P("band", "mp"),
        P("band", None),
        P("band"),
    )
    return jax.shard_map(
        local,
        mesh=mesh,
        in_specs=placed,
        out_specs=(P("band", "mp"), P(None, "mp"), P(None, "mp")),
        check_vma=False,
    )
```

```python
import jax
import jax.numpy as jnp
from jax import lax
from jax.experimental import pallas as pl
from jax.experimental.pallas import tpu as pltpu
from jax.sharding import PartitionSpec as P

REACH = 2
NEAR = 2 * REACH + 1
OWNER_BLOCKS = 2
SLOTS = 4

FL, BF = jnp.float32, jnp.bfloat16
ROWS_BY_ROWS = (((0,), (0,)), ((), ()))
COLS_BY_COLS = (((1,), (1,)), ((), ()))


def dot(left, right, dims=(((1,), (0,)), ((), ()))):
    return lax.dot_general(left, right, dims, preferred_element_type=FL)


def swap(value):
    return lax.ppermute(value, "mp", [(0, 1), (1, 0)])


def outward(value, steps):
    count = lax.axis_size("band")
    pairs = []
    for band in range(count - steps):
        pairs.append((2 * band, 2 * (band + steps)))
        pairs.append((2 * (band + steps) + 1, 2 * band + 1))
    return lax.ppermute(value, ("band", "mp"), pairs)


def place(pm, block, slot, facing):
    target = pm[slot, block]
    offset = target // OWNER_BLOCKS - lax.axis_index("band")
    along = jnp.where(lax.axis_index("mp") == 0, offset, -offset) * facing
    along = jnp.clip(along, -REACH, REACH)
    stored = jnp.where(along >= 0, along, REACH - along)
    return stored * OWNER_BLOCKS + target % OWNER_BLOCKS


def live_of(pc, block, slot):
    return jnp.where(slot < pc[block], 1.0, 0.0).astype(FL)


def split_slabs(total, own, mine, other):
    blocks = own.shape[0] // total.shape[1]
    own[...] = total[:blocks].reshape(own.shape).astype(own.dtype)
    mine[...] = total[blocks : 3 * blocks].reshape(mine.shape).astype(mine.dtype)
    other[...] = total[3 * blocks :].reshape(other.shape).astype(other.dtype)


def sigmoid(value):
    return 0.5 * jnp.tanh(0.5 * value) + 0.5


def fetch(pairs, sems):
    copies = [pltpu.make_async_copy(src, dst, sems.at[at]) for at, (src, dst) in enumerate(pairs)]
    for copy in copies:
        copy.start()
    return copies


def lift_kernel(a_hbm, g_hbm, w_hbm, pm_hbm, pc_hbm, a_ref, w_ref, x_ref, pm_ref, pc_ref, g_ref, sems):
    blocks, slots, rows, points = a_ref.shape
    pairs = slots * rows
    early = 2
    parts = []
    for start, size in ((0, early), (early, blocks - early)):
        points_at, blocks_at = pl.ds(start * points, size * points), pl.ds(start, size)
        parts.append((g_hbm.at[points_at], g_ref.at[points_at]))
        parts.append((a_hbm.at[blocks_at], a_ref.at[blocks_at]))
    copies = fetch([*parts, (w_hbm, w_ref), (pm_hbm, pm_ref), (pc_hbm, pc_ref)], sems)
    for copy in copies[:2]:
        copy.wait()
    for block in range(blocks):
        if block == early:
            for copy in copies[2:4]:
                copy.wait()
        weights = a_ref[block].reshape(pairs, points)
        x = dot(weights, g_ref[block * points : (block + 1) * points])
        x_ref[block * pairs : (block + 1) * pairs] = x.astype(BF)
    for copy in copies[4:]:
        copy.wait()


def by_side(w_ref):
    half = w_ref.shape[0] // 2
    core = lax.axis_index("mp")
    return [w_ref[pl.ds(pl.multiple_of(side * half, half), half)] for side in (core, 1 - core)]


def encode_kernel(
    pm, pc, a_ref, w_ref, x_own, g_other, x_other, own, mine, other, total
):
    blocks, slots, rows, points = a_ref.shape
    pairs = slots * rows
    w_own, w_far = by_side(w_ref)
    total[...] = jnp.zeros_like(total)
    for block in range(blocks):
        span = slice(block * pairs, (block + 1) * pairs)
        weights = a_ref[block].reshape(pairs, points)
        x = dot(weights, g_other[block * points : (block + 1) * points]).astype(BF)
        x_other[span] = x
        u = dot(x_own[span], w_own) + dot(x, w_far)
        for slot in range(slots):
            part = u[slot * rows : (slot + 1) * rows]
            sig = sigmoid(part)
            total[place(pm, block, slot, 1)] += part * sig * live_of(pc, block, slot)
    split_slabs(total, own, mine, other)


def slope_kernel(pc, w_ref, x_own, x_other, slope_ref):
    blocks = pc.shape[0]
    pairs = x_own.shape[0] // blocks
    rows = pairs // SLOTS
    w_own, w_far = by_side(w_ref)
    for block in range(blocks):
        span = slice(block * pairs, (block + 1) * pairs)
        u = dot(x_own[span], w_own) + dot(x_other[span], w_far)
        for slot in range(SLOTS):
            part = u[slot * rows : (slot + 1) * rows]
            sig = sigmoid(part)
            slope = (sig + part * sig * (1.0 - sig)) * (0.25 * live_of(pc, block, slot))
            slope_ref[block * pairs + slot * rows : block * pairs + (slot + 1) * rows] = slope.astype(BF)


def gather_near(near, refs, picks):
    blocks = near.shape[0] // len(refs)
    rows, width = near.shape[1], near.shape[2] // 2

    def fill(own_at):
        for at, (ref, pick) in enumerate(zip(refs, picks)):
            for half in range(2):
                column = (own_at + half) % 2 * width
                value = ref[half ^ pick].reshape(blocks, rows, width)
                near[at * blocks : (at + 1) * blocks, :, column : column + width] = value

    core = lax.axis_index("mp")
    pl.when(core == 0)(lambda: fill(0))
    pl.when(core == 1)(lambda: fill(1))


def decode_kernel(
    pm, pc, a_ref, g_ref, cot_ref, w_ref, m, q1, q2, t1, t2,
    out_ref, y_ref, dz_ref, own, mine, other, near, total,
):
    blocks, slots, rows, points = a_ref.shape
    pairs = slots * points
    total[...] = jnp.zeros_like(total)
    gather_near(near, (m, q1, q2, t1, t2), (0, 0, 0, 1, 1))
    for block in range(blocks):
        for slot in range(slots):
            chosen = near[place(pm, block, slot, -1)]
            y = dot(a_ref[block, slot], chosen, ROWS_BY_ROWS).astype(BF)
            y_ref[block * pairs + slot * points : block * pairs + (slot + 1) * points] = y
        span = slice(block * points, (block + 1) * points)
        z = dot(y_ref[block * pairs : (block + 1) * pairs], w_ref[...])
        result = g_ref[span].astype(FL)
        upstream = cot_ref[span].astype(FL)
        for slot in range(slots):
            part = z[slot * points : (slot + 1) * points]
            sig = sigmoid(part)
            edge = part * sig
            live = live_of(pc, block, slot)
            result = result + edge * live
            slope = sig + edge * (1.0 - sig)
            dz = ((upstream * live) * slope).astype(BF)
            dz_ref[block * pairs + slot * points : block * pairs + (slot + 1) * points] = dz
        out_ref[span] = result.astype(BF)
    for block in range(blocks):
        for slot in range(slots):
            dz = dz_ref[block * pairs + slot * points : block * pairs + (slot + 1) * points]
            total[place(pm, block, slot, 1)] += dot(a_ref[block, slot], dz)
    split_slabs(total, own, mine, other)


def outer_kernel(left_ref, right_ref, made_ref, out_ref, sent_ref):
    out_ref[...] = dot(right_ref[...], left_ref[...], ROWS_BY_ROWS)
    sent_ref[...] = made_ref[...]


def mesh_grad_kernel(s, t, w_own, w_other, out):
    half = out.shape[2]
    lift_own = (s[0].astype(FL) + t[1].astype(FL)).astype(BF)
    lift_other = (s[1].astype(FL) + t[0].astype(FL)).astype(BF)
    grad = dot(lift_own, w_own[...], COLS_BY_COLS) + dot(lift_other, w_other[...], COLS_BY_COLS)
    grad = grad.astype(BF)
    core = lax.axis_index("mp")

    @pl.when(core == 0)
    def _():
        out[0], out[1] = grad[:, :half], grad[:, half:]

    @pl.when(core == 1)
    def _():
        out[0], out[1] = grad[:, half:], grad[:, :half]


def encoder_grad_kernel(
    pm, pc, x_own, x_other, slope_ref, m, q1, q2, t1, t2, dec_ref, out_ref, near, total
):
    slots, blocks = pm.shape
    rows = near.shape[1]
    pairs = slots * rows
    for at, ref in enumerate((m, q1, q2, t1, t2)):
        near[at * OWNER_BLOCKS : (at + 1) * OWNER_BLOCKS] = ref[at // 3].reshape(OWNER_BLOCKS, rows, -1)
    for block in range(blocks):
        parts = []
        for slot in range(slots):
            picked = near[place(pm, block, slot, -1)].astype(FL)
            start = block * pairs + slot * rows
            parts.append((picked * slope_ref[start : start + rows].astype(FL)).astype(BF))
        du = jnp.concatenate(parts, axis=0)
        for at, x_ref in enumerate((x_own, x_other)):
            term = dot(du, x_ref[block * pairs : (block + 1) * pairs], ROWS_BY_ROWS)
            total[at] = term if block == 0 else total[at] + term
    count, half = total.shape[1:]
    lanes = out_ref.shape[1]
    tiles = half // lanes

    def store(tile, value):
        out_ref[tile * count : (tile + 1) * count] = value.astype(BF)

    def store_encoder(order):
        for at, side in enumerate(order):
            for tile in range(tiles):
                store(at * tiles + tile, total[side, :, tile * lanes : (tile + 1) * lanes])

    core = lax.axis_index("mp")
    pl.when(core == 0)(lambda: store_encoder((0, 1)))
    pl.when(core == 1)(lambda: store_encoder((1, 0)))
    for tile in range(2 * tiles):
        store(2 * tiles + tile, dec_ref[:, tile * lanes : (tile + 1) * lanes])


def sum_kernel(parts_ref, out_ref):
    total = parts_ref[...].astype(FL).sum(axis=0).astype(BF)
    out_ref[...] = jnp.broadcast_to(total[None], out_ref.shape)


def finish_kernel(flat_ref, enc_ref, dec_ref):
    lanes = flat_ref.shape[1]
    width, count = enc_ref.shape
    for at, out in enumerate((enc_ref, dec_ref)):
        for tile in range(width // lanes):
            start = (at * width // lanes + tile) * count
            piece = flat_ref[start : start + count].astype(FL)
            out[tile * lanes : (tile + 1) * lanes] = piece.T


def plane_groups(count):
    across = min(16, count // 2)
    plane = [list(range(at, at + across)) for at in range(0, count, across)]
    line = [list(range(at, count, across)) for at in range(across)]
    return plane, line


def exchange(value, groups):
    return lax.all_to_all(value, "band", 0, 0, tiled=True, axis_index_groups=groups)


def params():
    return pltpu.CompilerParams(vmem_limit_bytes=24 * 2**20)


def shape_of(*shape, dtype=BF):
    return jax.ShapeDtypeStruct(shape, dtype)


def simple(kernel, out_shape):
    return pl.pallas_call(kernel, out_shape=out_shape, compiler_params=params())


def combine(own, parts):
    first, second = (part.astype(FL) for part in parts)
    total = first + second
    return jnp.stack([total[0] + own.astype(FL), total[1]]).astype(BF)


def reduce_to_owner(own, mine, other, beside=None):
    got = swap(other)
    parts = [outward(jnp.stack([mine[i], got[i]]), i + 1) for i in range(REACH)]
    parts, beside = lax.optimization_barrier((parts, beside))
    sums = combine(own, parts)
    return sums, swap(sums), beside


def spread_from_owner(value):
    near = [outward(value, i + 1) for i in range(REACH)]
    return [value, *near, *(swap(part) for part in near)]


VMEM, HBM, SMEM = (pl.BlockSpec(memory_space=space) for space in (pltpu.VMEM, pltpu.HBM, pltpu.SMEM))


def held(kernel, in_specs, out_shape, scratch=(), cost=None):
    return pl.pallas_call(
        kernel,
        in_specs=in_specs,
        out_specs=jax.tree.map(lambda _: VMEM, out_shape),
        out_shape=out_shape,
        scratch_shapes=scratch,
        compiler_params=params(),
        cost_estimate=cost,
    )


def slab_shapes(owner_rows, half):
    return [shape_of(*lead, owner_rows, half) for lead in ((), (REACH,), (REACH,))]


def lift_own(*given):
    interp, grid, w_enc, pair_mesh, pair_count = given
    blocks, slots, rows, points = interp.shape
    half = w_enc.shape[1]
    pairs = blocks * slots * rows
    cost = pl.CostEstimate(flops=2 * pairs * points * half, bytes_accessed=4 * 2**20, transcendentals=0)
    fixed = [jax.ShapeDtypeStruct(value.shape, value.dtype) for value in (pair_mesh, pair_count)]
    return pl.pallas_call(
        lift_kernel,
        in_specs=[HBM] * 5,
        out_specs=[VMEM, VMEM, VMEM, SMEM, SMEM],
        out_shape=[shape_of(*interp.shape), shape_of(*w_enc.shape), shape_of(pairs, half), *fixed],
        scratch_shapes=[pltpu.VMEM(grid.shape, BF), pltpu.SemaphoreType.DMA((7,))],
        compiler_params=params(),
        cost_estimate=cost,
    )(*(pltpu.with_memory_space_constraint(value, pltpu.HBM) for value in given))


def encode(pair_mesh, pair_count, interp, w_enc, x_own, grid_other):
    blocks, slots, rows, points = interp.shape
    pairs, half = x_own.shape
    return held(
        encode_kernel,
        [SMEM, SMEM, *[VMEM] * 4],
        [shape_of(pairs, half), *slab_shapes(OWNER_BLOCKS * rows, half)],
        [pltpu.VMEM((NEAR * OWNER_BLOCKS, rows, half), FL)],
    )(pair_mesh, pair_count, interp, w_enc, x_own, grid_other)


def slopes(pair_count, w_enc, x_own, x_other):
    pairs, half = x_own.shape
    cost = pl.CostEstimate(
        flops=4 * pairs * half * half, bytes_accessed=6 * pairs * half, transcendentals=pairs * half
    )
    return held(slope_kernel, [SMEM, *[VMEM] * 3], shape_of(pairs, half), cost=cost)(
        pair_count, w_enc, x_own, x_other
    )


def decode(pair_mesh, pair_count, interp, grid, cotangent, w_dec, near):
    blocks, slots, rows, points = interp.shape
    full, half = w_dec.shape
    pairs = blocks * slots * points
    return held(
        decode_kernel,
        [SMEM, SMEM, *[VMEM] * (4 + NEAR)],
        [
            shape_of(*grid.shape), shape_of(pairs, full), shape_of(pairs, half),
            *slab_shapes(OWNER_BLOCKS * rows, half),
        ],
        [
            pltpu.VMEM((NEAR * OWNER_BLOCKS, rows, full), BF),
            pltpu.VMEM((NEAR * OWNER_BLOCKS, rows, half), FL),
        ],
    )(pair_mesh, pair_count, interp, grid, cotangent, w_dec, *near)


def outer(y, dz, made):
    pairs, full = y.shape
    half = dz.shape[1]
    cost = pl.CostEstimate(
        flops=2 * pairs * full * half, bytes_accessed=2 * pairs * (full + half), transcendentals=0
    )
    outs = [shape_of(half, full, dtype=FL), shape_of(*made.shape)]
    return held(outer_kernel, [VMEM] * 3, outs, cost=cost)(y, dz, made)


def encoder_grad(pair_mesh, pair_count, x_own, x_other, slope, near, grad_dec):
    half = slope.shape[1]
    rows = near[0].shape[1] // OWNER_BLOCKS
    return held(
        encoder_grad_kernel,
        [SMEM, SMEM, *[VMEM] * (4 + NEAR)],
        shape_of(8 * half, half // 2),
        [pltpu.VMEM((NEAR * OWNER_BLOCKS, rows, half), BF), pltpu.VMEM((2, half, half), FL)],
    )(pair_mesh, pair_count, x_own, x_other, slope, *near, grad_dec)


def local(grid, interp, mesh_init, w_enc, w_dec, cotangent, pair_mesh, pair_count):
    full, half = w_enc.shape
    pair_mesh = pair_mesh.T
    grid_other = swap(grid)
    mesh_both = jnp.stack([mesh_init, swap(mesh_init)])
    w_dec_other = swap(w_dec)

    interp, w_enc, x_own, pair_mesh, pair_count = lift_own(interp, grid, w_enc, pair_mesh, pair_count)
    x_other, own, mine, other = encode(pair_mesh, pair_count, interp, w_enc, x_own, grid_other)
    slope = slopes(pair_count, w_enc, x_own, x_other)
    sums, got, slope = reduce_to_owner(own, mine, other, slope)
    agg = sums.astype(FL) + got.astype(FL)[::-1]
    mesh_lat = (mesh_both.astype(FL) + 0.25 * agg).astype(BF)
    near = spread_from_owner(mesh_lat)

    out, y, dz, own, mine, other = decode(
        pair_mesh, pair_count, interp, grid, cotangent, w_dec, near
    )
    sums, got, (grad_dec, out) = reduce_to_owner(own, mine, other, outer(y, dz, out))
    grad_mesh = simple(mesh_grad_kernel, shape_of(*sums.shape))(sums, got, w_dec, w_dec_other)
    near = spread_from_owner(grad_mesh)
    flat = encoder_grad(pair_mesh, pair_count, x_own, x_other, slope, near, grad_dec)

    plane, line = plane_groups(lax.axis_size("band"))
    across = len(plane[0])
    chunks = exchange(flat.reshape(across, -1, half // 2), plane)
    piece = simple(sum_kernel, shape_of(len(line[0]), *chunks.shape[1:]))(chunks)
    pieces = exchange(piece, line)
    spread = simple(sum_kernel, shape_of(*chunks.shape))(pieces)
    flat = exchange(spread, plane).reshape(flat.shape)
    grads = [shape_of(full, half, dtype=FL)] * 2
    grad_enc, grad_dec = simple(finish_kernel, grads)(flat)
    return (out, grad_enc, grad_dec)


def solution(mesh):
    placed = (
        P("band", "mp"),
        P("band", None, None, None),
        P("band", "mp"),
        P(None, "mp"),
        P(None, "mp"),
        P("band", "mp"),
        P("band", None),
        P("band"),
    )
    return jax.shard_map(
        local,
        mesh=mesh,
        in_specs=placed,
        out_specs=(P("band", "mp"), P(None, "mp"), P(None, "mp")),
        check_vma=False,
    )
```

```python
import jax
import jax.numpy as jnp
from jax import lax
from jax.experimental import pallas as pl
from jax.experimental.pallas import tpu as pltpu
from jax.sharding import PartitionSpec as P

REACH = 2
NEAR = 2 * REACH + 1
OWNER_BLOCKS = 2
SLOTS = 4
LEAST, USUAL = 2, 3

FL, BF = jnp.float32, jnp.bfloat16
ROWS_BY_ROWS = (((0,), (0,)), ((), ()))
COLS_BY_COLS = (((1,), (1,)), ((), ()))


def dot(left, right, dims=(((1,), (0,)), ((), ()))):
    return lax.dot_general(left, right, dims, preferred_element_type=FL)


def swap(value):
    return lax.ppermute(value, "mp", [(0, 1), (1, 0)])


def outward(value, steps):
    count = lax.axis_size("band")
    pairs = []
    for band in range(count - steps):
        pairs.append((2 * band, 2 * (band + steps)))
        pairs.append((2 * (band + steps) + 1, 2 * band + 1))
    return lax.ppermute(value, ("band", "mp"), pairs)


def place(pm, block, slot, facing):
    target = pm[slot, block]
    offset = target // OWNER_BLOCKS - lax.axis_index("band")
    along = jnp.where(lax.axis_index("mp") == 0, offset, -offset) * facing
    along = jnp.clip(along, -REACH, REACH)
    stored = jnp.where(along >= 0, along, REACH - along)
    return stored * OWNER_BLOCKS + target % OWNER_BLOCKS


def live_of(pc, block, slot):
    return jnp.where(slot < pc[block], 1.0, 0.0).astype(FL)


def largest(pc):
    most = pc[0]
    for block in range(1, pc.shape[0]):
        most = jnp.maximum(most, pc[block])
    return most


def by_count(pc, slots, body):
    most = largest(pc)
    for used in range(LEAST, slots + 1):
        fits = most <= used if used == LEAST else (most >= used if used == slots else most == used)
        pl.when(fits)(lambda used=used: body(used))


def split_slabs(total, own, mine, other):
    blocks = own.shape[0] // total.shape[1]
    own[...] = total[:blocks].reshape(own.shape).astype(own.dtype)
    mine[...] = total[blocks : 3 * blocks].reshape(mine.shape).astype(mine.dtype)
    other[...] = total[3 * blocks :].reshape(other.shape).astype(other.dtype)


def sigmoid(value):
    return 0.5 * jnp.tanh(0.5 * value) + 0.5


def fetch(pairs, sems):
    copies = [pltpu.make_async_copy(src, dst, sems.at[at]) for at, (src, dst) in enumerate(pairs)]
    for copy in copies:
        copy.start()
    return copies


def lift_kernel(a_hbm, g_hbm, w_hbm, pm_hbm, pc_hbm, a_ref, w_ref, x_ref, pm_ref, pc_ref, g_ref, sems):
    blocks, slots, rows, points = a_ref.shape
    pairs = slots * rows
    early = 2
    parts = []
    for start, size in ((0, early), (early, blocks - early)):
        points_at, blocks_at = pl.ds(start * points, size * points), pl.ds(start, size)
        parts.append((g_hbm.at[points_at], g_ref.at[points_at]))
        parts.append((a_hbm.at[blocks_at], a_ref.at[blocks_at]))
    copies = fetch([*parts, (w_hbm, w_ref), (pm_hbm, pm_ref), (pc_hbm, pc_ref)], sems)
    copies[-1].wait()
    for copy in copies[:2]:
        copy.wait()

    def body(used):
        for block in range(blocks):
            if block == early:
                for copy in copies[2:4]:
                    copy.wait()
            weights = a_ref[block, :used].reshape(used * rows, points)
            x = dot(weights, g_ref[block * points : (block + 1) * points])
            x_ref[block * pairs : block * pairs + used * rows] = x.astype(BF)

    by_count(pc_ref, slots, body)
    for copy in copies[4:-1]:
        copy.wait()


def by_side(w_ref):
    half = w_ref.shape[0] // 2
    core = lax.axis_index("mp")
    return [w_ref[pl.ds(pl.multiple_of(side * half, half), half)] for side in (core, 1 - core)]


def encode_kernel(
    pm, pc, a_ref, w_ref, x_own, g_other, x_other, own, mine, other, total
):
    blocks, slots, rows, points = a_ref.shape
    pairs = slots * rows
    total[...] = jnp.zeros_like(total)

    def body(used):
        w_own, w_far = by_side(w_ref)
        for block in range(blocks):
            span = slice(block * pairs, block * pairs + used * rows)
            weights = a_ref[block, :used].reshape(used * rows, points)
            x = dot(weights, g_other[block * points : (block + 1) * points]).astype(BF)
            x_other[span] = x
            u = dot(x_own[span], w_own) + dot(x, w_far)
            for slot in range(used):
                part = u[slot * rows : (slot + 1) * rows]
                sig = sigmoid(part)
                total[place(pm, block, slot, 1)] += part * sig * live_of(pc, block, slot)

    by_count(pc, slots, body)
    split_slabs(total, own, mine, other)


def slope_kernel(pc, w_ref, x_own, x_other, slope_ref):
    blocks = pc.shape[0]
    pairs = x_own.shape[0] // blocks
    rows = pairs // SLOTS

    def body(used):
        w_own, w_far = by_side(w_ref)
        for block in range(blocks):
            span = slice(block * pairs, block * pairs + used * rows)
            u = dot(x_own[span], w_own) + dot(x_other[span], w_far)
            for slot in range(used):
                part = u[slot * rows : (slot + 1) * rows]
                sig = sigmoid(part)
                slope = (sig + part * sig * (1.0 - sig)) * (0.25 * live_of(pc, block, slot))
                at = block * pairs + slot * rows
                slope_ref[at : at + rows] = slope.astype(BF)

    by_count(pc, SLOTS, body)


def gather_near(near, refs, picks):
    blocks = near.shape[0] // len(refs)
    rows, width = near.shape[1], near.shape[2] // 2

    def fill(own_at):
        for at, (ref, pick) in enumerate(zip(refs, picks)):
            for half in range(2):
                column = (own_at + half) % 2 * width
                value = ref[half ^ pick].reshape(blocks, rows, width)
                near[at * blocks : (at + 1) * blocks, :, column : column + width] = value

    core = lax.axis_index("mp")
    pl.when(core == 0)(lambda: fill(0))
    pl.when(core == 1)(lambda: fill(1))


def decode_kernel(
    pm, pc, a_ref, g_ref, cot_ref, w_ref, m, q1, q2, t1, t2,
    out_ref, y_ref, dz_ref, own, mine, other, near, total,
):
    blocks, slots, rows, points = a_ref.shape
    pairs = slots * points
    total[...] = jnp.zeros_like(total)
    gather_near(near, (m, q1, q2, t1, t2), (0, 0, 0, 1, 1))

    def lat(block, slot):
        at = block * pairs + slot * points
        return pl.ds(at if isinstance(block, int) else pl.multiple_of(at, points), points)

    def points_of(block):
        at = block * points
        return pl.ds(at if isinstance(block, int) else pl.multiple_of(at, points), points)

    def forward(block, first, last):
        for slot in range(first, last):
            chosen = near[place(pm, block, slot, -1)]
            y_ref[lat(block, slot)] = dot(a_ref[block, slot], chosen, ROWS_BY_ROWS).astype(BF)
        span = points_of(block)
        z = dot(y_ref[pl.ds(lat(block, first).start, (last - first) * points)], w_ref[...])
        result = (out_ref[span] if first else g_ref[span]).astype(FL)
        upstream = cot_ref[span].astype(FL)
        for slot in range(first, last):
            part = z[(slot - first) * points : (slot - first + 1) * points]
            sig = sigmoid(part)
            edge = part * sig
            live = live_of(pc, block, slot)
            result = result + edge * live
            slope = sig + edge * (1.0 - sig)
            dz_ref[lat(block, slot)] = ((upstream * live) * slope).astype(BF)
        out_ref[span] = result

    def backward(block, first, last):
        for slot in range(first, last):
            lift = dot(a_ref[block, slot], dz_ref[lat(block, slot)])
            total[place(pm, block, slot, 1)] += lift

    def body(used):
        for step in (forward, backward):
            for block in range(blocks):
                step(block, 0, used)

    def rest(block, _):
        for slot in range(USUAL, slots):
            live = slot < pc[block]

            @pl.when(live)
            def _(slot=slot):
                forward(block, slot, slot + 1)
                backward(block, slot, slot + 1)

            @pl.when(jnp.logical_not(live))
            def _(slot=slot):
                y_ref[lat(block, slot)] = jnp.zeros((points, y_ref.shape[1]), BF)
                dz_ref[lat(block, slot)] = jnp.zeros((points, dz_ref.shape[1]), BF)

    most = largest(pc)
    pl.when(most <= LEAST)(lambda: body(LEAST))
    pl.when(most > LEAST)(lambda: body(USUAL))
    pl.when(most > USUAL)(lambda: lax.fori_loop(0, blocks, rest, None))
    split_slabs(total, own, mine, other)


def outer_kernel(pc, left_ref, right_ref, made_ref, out_ref, sent_ref):
    blocks = pc.shape[0]
    pairs = left_ref.shape[0] // blocks
    rows = pairs // SLOTS

    def body(used):
        if used == SLOTS:
            out_ref[...] = dot(right_ref[...], left_ref[...], ROWS_BY_ROWS)
            return
        for block in range(blocks):
            span = slice(block * pairs, block * pairs + used * rows)
            term = dot(right_ref[span], left_ref[span], ROWS_BY_ROWS)
            out_ref[...] = term if block == 0 else out_ref[...] + term

    by_count(pc, SLOTS, body)
    sent_ref[...] = made_ref[...].astype(BF)


def mesh_grad_kernel(s, t, w_own, w_other, out):
    half = out.shape[2]
    lift_own = (s[0].astype(FL) + t[1].astype(FL)).astype(BF)
    lift_other = (s[1].astype(FL) + t[0].astype(FL)).astype(BF)
    grad = dot(lift_own, w_own[...], COLS_BY_COLS) + dot(lift_other, w_other[...], COLS_BY_COLS)
    grad = grad.astype(BF)
    core = lax.axis_index("mp")

    @pl.when(core == 0)
    def _():
        out[0], out[1] = grad[:, :half], grad[:, half:]

    @pl.when(core == 1)
    def _():
        out[0], out[1] = grad[:, half:], grad[:, :half]


def encoder_grad_kernel(
    pm, pc, x_own, x_other, slope_ref, m, q1, q2, t1, t2, dec_ref, out_ref, near, total
):
    slots, blocks = pm.shape
    rows = near.shape[1]
    pairs = slots * rows
    for at, ref in enumerate((m, q1, q2, t1, t2)):
        near[at * OWNER_BLOCKS : (at + 1) * OWNER_BLOCKS] = ref[at // 3].reshape(OWNER_BLOCKS, rows, -1)

    def body(used):
        for block in range(blocks):
            parts = []
            for slot in range(used):
                picked = near[place(pm, block, slot, -1)].astype(FL)
                start = block * pairs + slot * rows
                parts.append((picked * slope_ref[start : start + rows].astype(FL)).astype(BF))
            du = jnp.concatenate(parts, axis=0)
            for at, x_ref in enumerate((x_own, x_other)):
                term = dot(du, x_ref[block * pairs : block * pairs + used * rows], ROWS_BY_ROWS)
                total[at] = term if block == 0 else total[at] + term

    by_count(pc, slots, body)
    count, half = total.shape[1:]
    lanes = out_ref.shape[1]
    tiles = half // lanes

    def store(tile, value):
        out_ref[tile * count : (tile + 1) * count] = value.astype(BF)

    def store_encoder(order):
        for at, side in enumerate(order):
            for tile in range(tiles):
                store(at * tiles + tile, total[side, :, tile * lanes : (tile + 1) * lanes])

    core = lax.axis_index("mp")
    pl.when(core == 0)(lambda: store_encoder((0, 1)))
    pl.when(core == 1)(lambda: store_encoder((1, 0)))
    for tile in range(2 * tiles):
        store(2 * tiles + tile, dec_ref[:, tile * lanes : (tile + 1) * lanes])


def sum_kernel(parts_ref, out_ref):
    total = parts_ref[...].astype(FL).sum(axis=0).astype(BF)
    out_ref[...] = jnp.broadcast_to(total[None], out_ref.shape)


def finish_kernel(flat_ref, enc_ref, dec_ref):
    lanes = flat_ref.shape[1]
    width, count = enc_ref.shape
    for at, out in enumerate((enc_ref, dec_ref)):
        for tile in range(width // lanes):
            start = (at * width // lanes + tile) * count
            piece = flat_ref[start : start + count].astype(FL)
            out[tile * lanes : (tile + 1) * lanes] = piece.T


def plane_groups(count):
    across = min(16, count // 2)
    plane = [list(range(at, at + across)) for at in range(0, count, across)]
    line = [list(range(at, count, across)) for at in range(across)]
    return plane, line


def exchange(value, groups):
    return lax.all_to_all(value, "band", 0, 0, tiled=True, axis_index_groups=groups)


def params():
    return pltpu.CompilerParams(vmem_limit_bytes=24 * 2**20)


def shape_of(*shape, dtype=BF):
    return jax.ShapeDtypeStruct(shape, dtype)


def simple(kernel, out_shape):
    return pl.pallas_call(kernel, out_shape=out_shape, compiler_params=params())


def combine(own, parts):
    first, second = (part.astype(FL) for part in parts)
    total = first + second
    return jnp.stack([total[0] + own.astype(FL), total[1]]).astype(BF)


def reduce_to_owner(own, mine, other, beside=None):
    got = swap(other)
    parts = [outward(jnp.stack([mine[i], got[i]]), i + 1) for i in range(REACH)]
    parts, beside = lax.optimization_barrier((parts, beside))
    sums = combine(own, parts)
    return sums, swap(sums), beside


def spread_from_owner(value):
    near = [outward(value, i + 1) for i in range(REACH)]
    return [value, *near, *(swap(part) for part in near)]


VMEM, HBM, SMEM = (pl.BlockSpec(memory_space=space) for space in (pltpu.VMEM, pltpu.HBM, pltpu.SMEM))


def held(kernel, in_specs, out_shape, scratch=(), cost=None):
    return pl.pallas_call(
        kernel,
        in_specs=in_specs,
        out_specs=jax.tree.map(lambda _: VMEM, out_shape),
        out_shape=out_shape,
        scratch_shapes=scratch,
        compiler_params=params(),
        cost_estimate=cost,
    )


def slab_shapes(owner_rows, half):
    return [shape_of(*lead, owner_rows, half) for lead in ((), (REACH,), (REACH,))]


def lift_own(*given):
    interp, grid, w_enc, pair_mesh, pair_count = given
    blocks, slots, rows, points = interp.shape
    half = w_enc.shape[1]
    pairs = blocks * slots * rows
    cost = pl.CostEstimate(flops=2 * pairs * points * half, bytes_accessed=4 * 2**20, transcendentals=0)
    fixed = [jax.ShapeDtypeStruct(value.shape, value.dtype) for value in (pair_mesh, pair_count)]
    return pl.pallas_call(
        lift_kernel,
        in_specs=[HBM] * 5,
        out_specs=[VMEM, VMEM, VMEM, SMEM, SMEM],
        out_shape=[shape_of(*interp.shape), shape_of(*w_enc.shape), shape_of(pairs, half), *fixed],
        scratch_shapes=[pltpu.VMEM(grid.shape, BF), pltpu.SemaphoreType.DMA((7,))],
        compiler_params=params(),
        cost_estimate=cost,
    )(*(pltpu.with_memory_space_constraint(value, pltpu.HBM) for value in given))


def encode(pair_mesh, pair_count, interp, w_enc, x_own, grid_other):
    blocks, slots, rows, points = interp.shape
    pairs, half = x_own.shape
    return held(
        encode_kernel,
        [SMEM, SMEM, *[VMEM] * 4],
        [shape_of(pairs, half), *slab_shapes(OWNER_BLOCKS * rows, half)],
        [pltpu.VMEM((NEAR * OWNER_BLOCKS, rows, half), FL)],
    )(pair_mesh, pair_count, interp, w_enc, x_own, grid_other)


def slopes(pair_count, w_enc, x_own, x_other):
    pairs, half = x_own.shape
    cost = pl.CostEstimate(
        flops=4 * pairs * half * half, bytes_accessed=6 * pairs * half, transcendentals=pairs * half
    )
    return held(slope_kernel, [SMEM, *[VMEM] * 3], shape_of(pairs, half), cost=cost)(
        pair_count, w_enc, x_own, x_other
    )


def decode(pair_mesh, pair_count, interp, grid, cotangent, w_dec, near):
    blocks, slots, rows, points = interp.shape
    full, half = w_dec.shape
    pairs = blocks * slots * points
    return held(
        decode_kernel,
        [SMEM, SMEM, *[VMEM] * (4 + NEAR)],
        [
            shape_of(*grid.shape, dtype=FL), shape_of(pairs, full), shape_of(pairs, half),
            *slab_shapes(OWNER_BLOCKS * rows, half),
        ],
        [
            pltpu.VMEM((NEAR * OWNER_BLOCKS, rows, full), BF),
            pltpu.VMEM((NEAR * OWNER_BLOCKS, rows, half), FL),
        ],
    )(pair_mesh, pair_count, interp, grid, cotangent, w_dec, *near)


def outer(pair_count, y, dz, made):
    pairs, full = y.shape
    half = dz.shape[1]
    cost = pl.CostEstimate(
        flops=2 * pairs * full * half, bytes_accessed=2 * pairs * (full + half), transcendentals=0
    )
    outs = [shape_of(half, full, dtype=FL), shape_of(*made.shape)]
    return held(outer_kernel, [SMEM, *[VMEM] * 3], outs, cost=cost)(pair_count, y, dz, made)


def encoder_grad(pair_mesh, pair_count, x_own, x_other, slope, near, grad_dec):
    half = slope.shape[1]
    rows = near[0].shape[1] // OWNER_BLOCKS
    return held(
        encoder_grad_kernel,
        [SMEM, SMEM, *[VMEM] * (4 + NEAR)],
        shape_of(8 * half, half // 2),
        [pltpu.VMEM((NEAR * OWNER_BLOCKS, rows, half), BF), pltpu.VMEM((2, half, half), FL)],
    )(pair_mesh, pair_count, x_own, x_other, slope, *near, grad_dec)


def local(grid, interp, mesh_init, w_enc, w_dec, cotangent, pair_mesh, pair_count):
    full, half = w_enc.shape
    pair_mesh = pair_mesh.T
    grid_other = swap(grid)
    mesh_both = jnp.stack([mesh_init, swap(mesh_init)])
    w_dec_other = swap(w_dec)

    interp, w_enc, x_own, pair_mesh, pair_count = lift_own(interp, grid, w_enc, pair_mesh, pair_count)
    x_other, own, mine, other = encode(pair_mesh, pair_count, interp, w_enc, x_own, grid_other)
    slope = slopes(pair_count, w_enc, x_own, x_other)
    sums, got, slope = reduce_to_owner(own, mine, other, slope)
    agg = sums.astype(FL) + got.astype(FL)[::-1]
    mesh_lat = (mesh_both.astype(FL) + 0.25 * agg).astype(BF)
    near = spread_from_owner(mesh_lat)

    out, y, dz, own, mine, other = decode(
        pair_mesh, pair_count, interp, grid, cotangent, w_dec, near
    )
    sums, got, (grad_dec, out) = reduce_to_owner(own, mine, other, outer(pair_count, y, dz, out))
    grad_mesh = simple(mesh_grad_kernel, shape_of(*sums.shape))(sums, got, w_dec, w_dec_other)
    near = spread_from_owner(grad_mesh)
    flat = encoder_grad(pair_mesh, pair_count, x_own, x_other, slope, near, grad_dec)

    plane, line = plane_groups(lax.axis_size("band"))
    across = len(plane[0])
    chunks = exchange(flat.reshape(across, -1, half // 2), plane)
    piece = simple(sum_kernel, shape_of(len(line[0]), *chunks.shape[1:]))(chunks)
    pieces = exchange(piece, line)
    spread = simple(sum_kernel, shape_of(*chunks.shape))(pieces)
    flat = exchange(spread, plane).reshape(flat.shape)
    grads = [shape_of(full, half, dtype=FL)] * 2
    grad_enc, grad_dec = simple(finish_kernel, grads)(flat)
    return (out, grad_enc, grad_dec)


def solution(mesh):
    placed = (
        P("band", "mp"),
        P("band", None, None, None),
        P("band", "mp"),
        P(None, "mp"),
        P(None, "mp"),
        P("band", "mp"),
        P("band", None),
        P("band"),
    )
    return jax.shard_map(
        local,
        mesh=mesh,
        in_specs=placed,
        out_specs=(P("band", "mp"), P(None, "mp"), P(None, "mp")),
        check_vma=False,
    )
```

```python
import jax
import jax.numpy as jnp
from jax import lax
from jax.experimental import pallas as pl
from jax.experimental.pallas import tpu as pltpu
from jax.sharding import PartitionSpec as P

REACH = 2
NEAR = 2 * REACH + 1
OWNER_BLOCKS = 2
SLOTS = 4
LEAST, USUAL = 2, 3

FL, BF = jnp.float32, jnp.bfloat16
ROWS_BY_ROWS = (((0,), (0,)), ((), ()))
COLS_BY_COLS = (((1,), (1,)), ((), ()))


def dot(left, right, dims=(((1,), (0,)), ((), ()))):
    return lax.dot_general(left, right, dims, preferred_element_type=FL)


def swap(value):
    return lax.ppermute(value, "mp", [(0, 1), (1, 0)])


def outward(value, steps):
    count = lax.axis_size("band")
    pairs = []
    for band in range(count - steps):
        pairs.append((2 * band, 2 * (band + steps)))
        pairs.append((2 * (band + steps) + 1, 2 * band + 1))
    return lax.ppermute(value, ("band", "mp"), pairs)


def place(pm, block, slot, facing):
    target = pm[slot, block]
    offset = target // OWNER_BLOCKS - lax.axis_index("band")
    along = jnp.where(lax.axis_index("mp") == 0, offset, -offset) * facing
    along = jnp.clip(along, -REACH, REACH)
    stored = jnp.where(along >= 0, along, REACH - along)
    return stored * OWNER_BLOCKS + target % OWNER_BLOCKS


def live_of(pc, block, slot):
    return jnp.where(slot < pc[block], 1.0, 0.0).astype(FL)


def largest(pc):
    most = pc[0]
    for block in range(1, pc.shape[0]):
        most = jnp.maximum(most, pc[block])
    return most


def by_count(pc, slots, body):
    most = largest(pc)
    for used in range(LEAST, slots + 1):
        fits = most <= used if used == LEAST else (most >= used if used == slots else most == used)
        pl.when(fits)(lambda used=used: body(used))


def split_slabs(total, own, mine, other):
    blocks = own.shape[0] // total.shape[1]
    own[...] = total[:blocks].reshape(own.shape).astype(own.dtype)
    mine[...] = total[blocks : 3 * blocks].reshape(mine.shape).astype(mine.dtype)
    other[...] = total[3 * blocks :].reshape(other.shape).astype(other.dtype)


def sigmoid(value):
    return 0.5 * jnp.tanh(0.5 * value) + 0.5


def fetch(pairs, sems):
    copies = [pltpu.make_async_copy(src, dst, sems.at[at]) for at, (src, dst) in enumerate(pairs)]
    for copy in copies:
        copy.start()
    return copies


def lift_kernel(a_hbm, g_hbm, w_hbm, pm_hbm, pc_hbm, a_ref, w_ref, x_ref, pm_ref, pc_ref, g_ref, sems):
    blocks, slots, rows, points = a_ref.shape
    pairs = slots * rows
    early = 2
    parts = []
    for start, size in ((0, early), (early, blocks - early)):
        points_at, blocks_at = pl.ds(start * points, size * points), pl.ds(start, size)
        parts.append((g_hbm.at[points_at], g_ref.at[points_at]))
        parts.append((a_hbm.at[blocks_at], a_ref.at[blocks_at]))
    copies = fetch([*parts, (w_hbm, w_ref), (pm_hbm, pm_ref), (pc_hbm, pc_ref)], sems)
    copies[-1].wait()
    for copy in copies[:2]:
        copy.wait()

    def body(used):
        for block in range(blocks):
            if block == early:
                for copy in copies[2:4]:
                    copy.wait()
            weights = a_ref[block, :used].reshape(used * rows, points)
            x = dot(weights, g_ref[block * points : (block + 1) * points])
            x_ref[block * used * rows : (block + 1) * used * rows] = x.astype(BF)

    by_count(pc_ref, slots, body)
    for copy in copies[4:-1]:
        copy.wait()


def by_side(w_ref):
    half = w_ref.shape[0] // 2
    core = lax.axis_index("mp")
    return [w_ref[pl.ds(pl.multiple_of(side * half, half), half)] for side in (core, 1 - core)]


def encode_kernel(
    pm, pc, a_ref, w_ref, x_own, g_other, x_other, own, mine, other, total
):
    blocks, slots, rows, points = a_ref.shape
    pairs = slots * rows
    total[...] = jnp.zeros_like(total)

    def body(used):
        w_own, w_far = by_side(w_ref)
        for block in range(blocks):
            span = slice(block * used * rows, (block + 1) * used * rows)
            weights = a_ref[block, :used].reshape(used * rows, points)
            x = dot(weights, g_other[block * points : (block + 1) * points]).astype(BF)
            x_other[span] = x
            u = dot(x_own[span], w_own) + dot(x, w_far)
            for slot in range(used):
                part = u[slot * rows : (slot + 1) * rows]
                sig = sigmoid(part)
                total[place(pm, block, slot, 1)] += part * sig * live_of(pc, block, slot)

    by_count(pc, slots, body)
    split_slabs(total, own, mine, other)


def slope_kernel(pc, w_ref, x_own, x_other, slope_ref):
    blocks = pc.shape[0]
    pairs = x_own.shape[0] // blocks
    rows = pairs // SLOTS

    def body(used):
        w_own, w_far = by_side(w_ref)
        for block in range(blocks):
            span = slice(block * used * rows, (block + 1) * used * rows)
            u = dot(x_own[span], w_own) + dot(x_other[span], w_far)
            for slot in range(used):
                part = u[slot * rows : (slot + 1) * rows]
                sig = sigmoid(part)
                slope = (sig + part * sig * (1.0 - sig)) * (0.25 * live_of(pc, block, slot))
                at = (block * used + slot) * rows
                slope_ref[at : at + rows] = slope.astype(BF)

    by_count(pc, SLOTS, body)


def gather_near(near, refs, picks):
    blocks = near.shape[0] // len(refs)
    rows, width = near.shape[1], near.shape[2] // 2

    def fill(own_at):
        for at, (ref, pick) in enumerate(zip(refs, picks)):
            for half in range(2):
                column = (own_at + half) % 2 * width
                value = ref[half ^ pick].reshape(blocks, rows, width)
                near[at * blocks : (at + 1) * blocks, :, column : column + width] = value

    core = lax.axis_index("mp")
    pl.when(core == 0)(lambda: fill(0))
    pl.when(core == 1)(lambda: fill(1))


def decode_kernel(
    pm, pc, a_ref, g_ref, cot_ref, w_ref, m, q1, q2, t1, t2,
    out_ref, y_ref, dz_ref, own, mine, other, near, total,
):
    blocks, slots, rows, points = a_ref.shape
    pairs = slots * points
    total[...] = jnp.zeros_like(total)
    gather_near(near, (m, q1, q2, t1, t2), (0, 0, 0, 1, 1))

    def lat(block, slot):
        at = block * pairs + slot * points
        return pl.ds(at if isinstance(block, int) else pl.multiple_of(at, points), points)

    def points_of(block):
        at = block * points
        return pl.ds(at if isinstance(block, int) else pl.multiple_of(at, points), points)

    def forward(block, first, last):
        for slot in range(first, last):
            chosen = near[place(pm, block, slot, -1)]
            y_ref[lat(block, slot)] = dot(a_ref[block, slot], chosen, ROWS_BY_ROWS).astype(BF)
        span = points_of(block)
        z = dot(y_ref[pl.ds(lat(block, first).start, (last - first) * points)], w_ref[...])
        result = (out_ref[span] if first else g_ref[span]).astype(FL)
        upstream = cot_ref[span].astype(FL)
        for slot in range(first, last):
            part = z[(slot - first) * points : (slot - first + 1) * points]
            sig = sigmoid(part)
            edge = part * sig
            live = live_of(pc, block, slot)
            result = result + edge * live
            slope = sig + edge * (1.0 - sig)
            dz_ref[lat(block, slot)] = ((upstream * live) * slope).astype(BF)
        out_ref[span] = result

    def backward(block, first, last):
        for slot in range(first, last):
            lift = dot(a_ref[block, slot], dz_ref[lat(block, slot)])
            total[place(pm, block, slot, 1)] += lift

    def body(used):
        for step in (forward, backward):
            for block in range(blocks):
                step(block, 0, used)

    def rest(block, _):
        for slot in range(USUAL, slots):
            live = slot < pc[block]

            @pl.when(live)
            def _(slot=slot):
                forward(block, slot, slot + 1)
                backward(block, slot, slot + 1)

            @pl.when(jnp.logical_not(live))
            def _(slot=slot):
                y_ref[lat(block, slot)] = jnp.zeros((points, y_ref.shape[1]), BF)
                dz_ref[lat(block, slot)] = jnp.zeros((points, dz_ref.shape[1]), BF)

    most = largest(pc)
    pl.when(most <= LEAST)(lambda: body(LEAST))
    pl.when(most > LEAST)(lambda: body(USUAL))
    pl.when(most > USUAL)(lambda: lax.fori_loop(0, blocks, rest, None))
    split_slabs(total, own, mine, other)


def outer_kernel(pc, left_ref, right_ref, made_ref, out_ref, sent_ref):
    blocks = pc.shape[0]
    pairs = left_ref.shape[0] // blocks
    rows = pairs // SLOTS

    def body(used):
        if used == SLOTS:
            out_ref[...] = dot(right_ref[...], left_ref[...], ROWS_BY_ROWS)
            return
        for block in range(blocks):
            span = slice(block * pairs, block * pairs + used * rows)
            term = dot(right_ref[span], left_ref[span], ROWS_BY_ROWS)
            out_ref[...] = term if block == 0 else out_ref[...] + term

    by_count(pc, SLOTS, body)
    sent_ref[...] = made_ref[...].astype(BF)


def mesh_grad_kernel(s, t, w_own, w_other, out):
    half = out.shape[2]
    lift_own = (s[0].astype(FL) + t[1].astype(FL)).astype(BF)
    lift_other = (s[1].astype(FL) + t[0].astype(FL)).astype(BF)
    grad = dot(lift_own, w_own[...], COLS_BY_COLS) + dot(lift_other, w_other[...], COLS_BY_COLS)
    grad = grad.astype(BF)
    core = lax.axis_index("mp")

    @pl.when(core == 0)
    def _():
        out[0], out[1] = grad[:, :half], grad[:, half:]

    @pl.when(core == 1)
    def _():
        out[0], out[1] = grad[:, half:], grad[:, :half]


def encoder_grad_kernel(
    pm, pc, x_own, x_other, slope_ref, m, q1, q2, t1, t2, dec_ref, out_ref, near, total
):
    slots, blocks = pm.shape
    rows = near.shape[1]
    for at, ref in enumerate((m, q1, q2, t1, t2)):
        half = ref[0] if at < 3 else ref[...]
        near[at * OWNER_BLOCKS : (at + 1) * OWNER_BLOCKS] = half.reshape(OWNER_BLOCKS, rows, -1)

    def body(used):
        for first in range(0, blocks, 2):
            last = min(first + 2, blocks)
            parts = []
            for block in range(first, last):
                for slot in range(used):
                    picked = near[place(pm, block, slot, -1)].astype(FL)
                    start = (block * used + slot) * rows
                    parts.append((picked * slope_ref[start : start + rows].astype(FL)).astype(BF))
            du = jnp.concatenate(parts, axis=0)
            for at, x_ref in enumerate((x_own, x_other)):
                term = dot(du, x_ref[first * used * rows : last * used * rows], ROWS_BY_ROWS)
                total[at] = term if first == 0 else total[at] + term

    by_count(pc, slots, body)
    count, half = total.shape[1:]
    lanes = out_ref.shape[1]
    tiles = half // lanes

    def store(tile, value):
        out_ref[tile * count : (tile + 1) * count] = value.astype(BF)

    def store_encoder(order):
        for at, side in enumerate(order):
            for tile in range(tiles):
                store(at * tiles + tile, total[side, :, tile * lanes : (tile + 1) * lanes])

    core = lax.axis_index("mp")
    pl.when(core == 0)(lambda: store_encoder((0, 1)))
    pl.when(core == 1)(lambda: store_encoder((1, 0)))
    for tile in range(2 * tiles):
        store(2 * tiles + tile, dec_ref[:, tile * lanes : (tile + 1) * lanes])


def sum_kernel(parts_ref, out_ref):
    total = parts_ref[...].astype(FL).sum(axis=0).astype(BF)
    out_ref[...] = jnp.broadcast_to(total[None], out_ref.shape)


def finish_kernel(flat_ref, enc_ref, dec_ref):
    lanes = flat_ref.shape[1]
    width, count = enc_ref.shape
    for at, out in enumerate((enc_ref, dec_ref)):
        for tile in range(width // lanes):
            start = (at * width // lanes + tile) * count
            piece = flat_ref[start : start + count].astype(FL)
            out[tile * lanes : (tile + 1) * lanes] = piece.T


def plane_groups(count):
    across = min(16, count // 2)
    plane = [list(range(at, at + across)) for at in range(0, count, across)]
    line = [list(range(at, count, across)) for at in range(across)]
    return plane, line


def exchange(value, groups):
    return lax.all_to_all(value, "band", 0, 0, tiled=True, axis_index_groups=groups)


def params():
    return pltpu.CompilerParams(vmem_limit_bytes=24 * 2**20)


def shape_of(*shape, dtype=BF):
    return jax.ShapeDtypeStruct(shape, dtype)


def simple(kernel, out_shape):
    return pl.pallas_call(kernel, out_shape=out_shape, compiler_params=params())


def combine(own, parts):
    first, second = (part.astype(FL) for part in parts)
    total = first + second
    return jnp.stack([total[0] + own.astype(FL), total[1]]).astype(BF)


def reduce_to_owner(own, mine, other, beside=None):
    got = swap(other)
    parts = [outward(jnp.stack([mine[i], got[i]]), i + 1) for i in range(REACH)]
    parts, beside = lax.optimization_barrier((parts, beside))
    sums = combine(own, parts)
    return sums, swap(sums), beside


def spread_from_owner(value, wanted=lambda part: part):
    near = [outward(value, i + 1) for i in range(REACH)]
    return [value, *near, *(swap(wanted(part)) for part in near)]


VMEM, HBM, SMEM = (pl.BlockSpec(memory_space=space) for space in (pltpu.VMEM, pltpu.HBM, pltpu.SMEM))


def held(kernel, in_specs, out_shape, scratch=(), cost=None):
    return pl.pallas_call(
        kernel,
        in_specs=in_specs,
        out_specs=jax.tree.map(lambda _: VMEM, out_shape),
        out_shape=out_shape,
        scratch_shapes=scratch,
        compiler_params=params(),
        cost_estimate=cost,
    )


def slab_shapes(owner_rows, half):
    return [shape_of(*lead, owner_rows, half) for lead in ((), (REACH,), (REACH,))]


def lift_own(*given):
    interp, grid, w_enc, pair_mesh, pair_count = given
    blocks, slots, rows, points = interp.shape
    half = w_enc.shape[1]
    pairs = blocks * slots * rows
    cost = pl.CostEstimate(flops=2 * pairs * points * half, bytes_accessed=4 * 2**20, transcendentals=0)
    fixed = [jax.ShapeDtypeStruct(value.shape, value.dtype) for value in (pair_mesh, pair_count)]
    return pl.pallas_call(
        lift_kernel,
        in_specs=[HBM] * 5,
        out_specs=[VMEM, VMEM, VMEM, SMEM, SMEM],
        out_shape=[shape_of(*interp.shape), shape_of(*w_enc.shape), shape_of(pairs, half), *fixed],
        scratch_shapes=[pltpu.VMEM(grid.shape, BF), pltpu.SemaphoreType.DMA((7,))],
        compiler_params=params(),
        cost_estimate=cost,
    )(*(pltpu.with_memory_space_constraint(value, pltpu.HBM) for value in given))


def encode(pair_mesh, pair_count, interp, w_enc, x_own, grid_other):
    blocks, slots, rows, points = interp.shape
    pairs, half = x_own.shape
    return held(
        encode_kernel,
        [SMEM, SMEM, *[VMEM] * 4],
        [shape_of(pairs, half), *slab_shapes(OWNER_BLOCKS * rows, half)],
        [pltpu.VMEM((NEAR * OWNER_BLOCKS, rows, half), FL)],
    )(pair_mesh, pair_count, interp, w_enc, x_own, grid_other)


def slopes(pair_count, w_enc, x_own, x_other):
    pairs, half = x_own.shape
    cost = pl.CostEstimate(
        flops=4 * pairs * half * half, bytes_accessed=6 * pairs * half, transcendentals=pairs * half
    )
    return held(slope_kernel, [SMEM, *[VMEM] * 3], shape_of(pairs, half), cost=cost)(
        pair_count, w_enc, x_own, x_other
    )


def decode(pair_mesh, pair_count, interp, grid, cotangent, w_dec, near):
    blocks, slots, rows, points = interp.shape
    full, half = w_dec.shape
    pairs = blocks * slots * points
    return held(
        decode_kernel,
        [SMEM, SMEM, *[VMEM] * (4 + NEAR)],
        [
            shape_of(*grid.shape, dtype=FL), shape_of(pairs, full), shape_of(pairs, half),
            *slab_shapes(OWNER_BLOCKS * rows, half),
        ],
        [
            pltpu.VMEM((NEAR * OWNER_BLOCKS, rows, full), BF),
            pltpu.VMEM((NEAR * OWNER_BLOCKS, rows, half), FL),
        ],
    )(pair_mesh, pair_count, interp, grid, cotangent, w_dec, *near)


def outer(pair_count, y, dz, made):
    pairs, full = y.shape
    half = dz.shape[1]
    cost = pl.CostEstimate(
        flops=2 * pairs * full * half, bytes_accessed=2 * pairs * (full + half), transcendentals=0
    )
    outs = [shape_of(half, full, dtype=FL), shape_of(*made.shape)]
    return held(outer_kernel, [SMEM, *[VMEM] * 3], outs, cost=cost)(pair_count, y, dz, made)


def encoder_grad(pair_mesh, pair_count, x_own, x_other, slope, near, grad_dec):
    half = slope.shape[1]
    rows = near[0].shape[1] // OWNER_BLOCKS
    return held(
        encoder_grad_kernel,
        [SMEM, SMEM, *[VMEM] * (4 + NEAR)],
        shape_of(8 * half, half // 2),
        [pltpu.VMEM((NEAR * OWNER_BLOCKS, rows, half), BF), pltpu.VMEM((2, half, half), FL)],
    )(pair_mesh, pair_count, x_own, x_other, slope, *near, grad_dec)


def local(grid, interp, mesh_init, w_enc, w_dec, cotangent, pair_mesh, pair_count):
    full, half = w_enc.shape
    pair_mesh = pair_mesh.T
    swapped = [swap(value) for value in (grid, mesh_init, w_dec)]
    grid_other, mesh_other, w_dec_other = lax.optimization_barrier(swapped)
    mesh_both = jnp.stack([mesh_init, mesh_other])

    interp, w_enc, x_own, pair_mesh, pair_count = lift_own(interp, grid, w_enc, pair_mesh, pair_count)
    x_other, own, mine, other = encode(pair_mesh, pair_count, interp, w_enc, x_own, grid_other)
    slope = slopes(pair_count, w_enc, x_own, x_other)
    sums, got, slope = reduce_to_owner(own, mine, other, slope)
    agg = sums.astype(FL) + got.astype(FL)[::-1]
    mesh_lat = (mesh_both.astype(FL) + 0.25 * agg).astype(BF)
    near = spread_from_owner(mesh_lat)

    out, y, dz, own, mine, other = decode(
        pair_mesh, pair_count, interp, grid, cotangent, w_dec, near
    )
    sums, got, (grad_dec, out) = reduce_to_owner(own, mine, other, outer(pair_count, y, dz, out))
    grad_mesh = simple(mesh_grad_kernel, shape_of(*sums.shape))(sums, got, w_dec, w_dec_other)
    near = spread_from_owner(grad_mesh, lambda part: part[1])
    flat = encoder_grad(pair_mesh, pair_count, x_own, x_other, slope, near, grad_dec)

    plane, line = plane_groups(lax.axis_size("band"))
    across = len(plane[0])
    chunks = exchange(flat.reshape(across, -1, half // 2), plane)
    piece = simple(sum_kernel, shape_of(len(line[0]), *chunks.shape[1:]))(chunks)
    pieces = exchange(piece, line)
    spread = simple(sum_kernel, shape_of(*chunks.shape))(pieces)
    flat = exchange(spread, plane).reshape(flat.shape)
    grads = [shape_of(full, half, dtype=FL)] * 2
    grad_enc, grad_dec = simple(finish_kernel, grads)(flat)
    return (out, grad_enc, grad_dec)


def solution(mesh):
    placed = (
        P("band", "mp"),
        P("band", None, None, None),
        P("band", "mp"),
        P(None, "mp"),
        P(None, "mp"),
        P("band", "mp"),
        P("band", None),
        P("band"),
    )
    return jax.shard_map(
        local,
        mesh=mesh,
        in_specs=placed,
        out_specs=(P("band", "mp"), P(None, "mp"), P(None, "mp")),
        check_vma=False,
    )
```

```python
import jax
import jax.numpy as jnp
from jax import lax
from jax.experimental import pallas as pl
from jax.experimental.pallas import tpu as pltpu
from jax.sharding import PartitionSpec as P

REACH = 2
NEAR = 2 * REACH + 1
OWNER_BLOCKS = 2
SLOTS = 4
LEAST, USUAL = 2, 3

FL, BF = jnp.float32, jnp.bfloat16
ROWS_BY_ROWS = (((0,), (0,)), ((), ()))
COLS_BY_COLS = (((1,), (1,)), ((), ()))


def dot(left, right, dims=(((1,), (0,)), ((), ()))):
    return lax.dot_general(left, right, dims, preferred_element_type=FL)


def swap(value):
    return lax.ppermute(value, "mp", [(0, 1), (1, 0)])


def outward(value, steps):
    count = lax.axis_size("band")
    pairs = []
    for band in range(count - steps):
        pairs.append((2 * band, 2 * (band + steps)))
        pairs.append((2 * (band + steps) + 1, 2 * band + 1))
    return lax.ppermute(value, ("band", "mp"), pairs)


def place(pm, block, slot, facing):
    target = pm[slot, block]
    offset = target // OWNER_BLOCKS - lax.axis_index("band")
    along = jnp.where(lax.axis_index("mp") == 0, offset, -offset) * facing
    along = jnp.clip(along, -REACH, REACH)
    stored = jnp.where(along >= 0, along, REACH - along)
    return stored * OWNER_BLOCKS + target % OWNER_BLOCKS


def live_of(pc, block, slot):
    return jnp.where(slot < pc[block], 1.0, 0.0).astype(FL)


def largest(pc):
    most = pc[0]
    for block in range(1, pc.shape[0]):
        most = jnp.maximum(most, pc[block])
    return most


def by_count(pc, slots, body):
    most = largest(pc)
    for used in range(LEAST, slots + 1):
        fits = most <= used if used == LEAST else (most >= used if used == slots else most == used)
        pl.when(fits)(lambda used=used: body(used))


def split_slabs(total, own, mine, other):
    blocks = own.shape[0] // total.shape[1]
    own[...] = total[:blocks].reshape(own.shape).astype(own.dtype)
    mine[...] = total[blocks : 3 * blocks].reshape(mine.shape).astype(mine.dtype)
    other[...] = total[3 * blocks :].reshape(other.shape).astype(other.dtype)


def sigmoid(value):
    return 0.5 * jnp.tanh(0.5 * value) + 0.5


def fetch(pairs, sems):
    copies = [pltpu.make_async_copy(src, dst, sems.at[at]) for at, (src, dst) in enumerate(pairs)]
    for copy in copies:
        copy.start()
    return copies


def lift_kernel(a_hbm, g_hbm, w_hbm, pm_hbm, pc_hbm, a_ref, w_ref, x_ref, pm_ref, pc_ref, g_ref, sems):
    blocks, slots, rows, points = a_ref.shape
    pairs = slots * rows
    early = 2
    parts = []
    for start, size in ((0, early), (early, blocks - early)):
        points_at, blocks_at = pl.ds(start * points, size * points), pl.ds(start, size)
        parts.append((g_hbm.at[points_at], g_ref.at[points_at]))
        parts.append((a_hbm.at[blocks_at], a_ref.at[blocks_at]))
    copies = fetch([*parts, (w_hbm, w_ref), (pm_hbm, pm_ref), (pc_hbm, pc_ref)], sems)
    copies[-1].wait()
    for copy in copies[:2]:
        copy.wait()

    def body(used):
        for block in range(blocks):
            if block == early:
                for copy in copies[2:4]:
                    copy.wait()
            weights = a_ref[block, :used].reshape(used * rows, points)
            x = dot(weights, g_ref[block * points : (block + 1) * points])
            x_ref[block * used * rows : (block + 1) * used * rows] = x.astype(BF)

    by_count(pc_ref, slots, body)
    for copy in copies[4:-1]:
        copy.wait()


def by_side(w_ref):
    half = w_ref.shape[0] // 2
    core = lax.axis_index("mp")
    return [w_ref[pl.ds(pl.multiple_of(side * half, half), half)] for side in (core, 1 - core)]


def encode_kernel(
    pm, pc, a_ref, w_ref, x_own, g_other, x_other, own, mine, other, total
):
    blocks, slots, rows, points = a_ref.shape
    pairs = slots * rows
    total[...] = jnp.zeros_like(total)

    def body(used):
        w_own, w_far = by_side(w_ref)
        for block in range(blocks):
            span = slice(block * used * rows, (block + 1) * used * rows)
            weights = a_ref[block, :used].reshape(used * rows, points)
            x = dot(weights, g_other[block * points : (block + 1) * points]).astype(BF)
            x_other[span] = x
            u = dot(x_own[span], w_own) + dot(x, w_far)
            for slot in range(used):
                part = u[slot * rows : (slot + 1) * rows]
                sig = sigmoid(part)
                total[place(pm, block, slot, 1)] += part * sig * live_of(pc, block, slot)

    by_count(pc, slots, body)
    split_slabs(total, own, mine, other)


def slope_kernel(pc, w_ref, x_own, x_other, slope_ref):
    blocks = pc.shape[0]
    pairs = x_own.shape[0] // blocks
    rows = pairs // SLOTS

    def body(used):
        w_own, w_far = by_side(w_ref)
        for block in range(blocks):
            span = slice(block * used * rows, (block + 1) * used * rows)
            u = dot(x_own[span], w_own) + dot(x_other[span], w_far)
            for slot in range(used):
                part = u[slot * rows : (slot + 1) * rows]
                sig = sigmoid(part)
                slope = (sig + part * sig * (1.0 - sig)) * (0.25 * live_of(pc, block, slot))
                at = (block * used + slot) * rows
                slope_ref[at : at + rows] = slope.astype(BF)

    by_count(pc, SLOTS, body)


def gather_near(near, refs, picks):
    blocks = near.shape[0] // len(refs)
    rows, width = near.shape[1], near.shape[2] // 2

    def fill(own_at):
        for at, (ref, pick) in enumerate(zip(refs, picks)):
            for half in range(2):
                column = (own_at + half) % 2 * width
                value = ref[half ^ pick].reshape(blocks, rows, width)
                near[at * blocks : (at + 1) * blocks, :, column : column + width] = value

    core = lax.axis_index("mp")
    pl.when(core == 0)(lambda: fill(0))
    pl.when(core == 1)(lambda: fill(1))


def decode_kernel(
    pm, pc, a_ref, g_ref, cot_ref, w_ref, m, q1, q2, t1, t2,
    out_ref, y_ref, dz_ref, own, mine, other, near, total,
):
    blocks, slots, rows, points = a_ref.shape
    pairs = slots * points
    total[...] = jnp.zeros_like(total)
    gather_near(near, (m, q1, q2, t1, t2), (0, 0, 0, 1, 1))

    def lat(block, slot):
        at = block * pairs + slot * points
        return pl.ds(at if isinstance(block, int) else pl.multiple_of(at, points), points)

    def points_of(block):
        at = block * points
        return pl.ds(at if isinstance(block, int) else pl.multiple_of(at, points), points)

    def forward(block, first, last):
        for slot in range(first, last):
            chosen = near[place(pm, block, slot, -1)]
            y_ref[lat(block, slot)] = dot(a_ref[block, slot], chosen, ROWS_BY_ROWS).astype(BF)
        span = points_of(block)
        z = dot(y_ref[pl.ds(lat(block, first).start, (last - first) * points)], w_ref[...])
        result = (out_ref[span] if first else g_ref[span]).astype(FL)
        upstream = cot_ref[span].astype(FL)
        for slot in range(first, last):
            part = z[(slot - first) * points : (slot - first + 1) * points]
            sig = sigmoid(part)
            edge = part * sig
            live = live_of(pc, block, slot)
            result = result + edge * live
            slope = sig + edge * (1.0 - sig)
            dz_ref[lat(block, slot)] = ((upstream * live) * slope).astype(BF)
        out_ref[span] = result

    def backward(block, first, last):
        for slot in range(first, last):
            lift = dot(a_ref[block, slot], dz_ref[lat(block, slot)])
            total[place(pm, block, slot, 1)] += lift

    def body(used):
        for step in (forward, backward):
            for block in range(blocks):
                step(block, 0, used)

    def rest(block, _):
        for slot in range(USUAL, slots):
            live = slot < pc[block]

            @pl.when(live)
            def _(slot=slot):
                forward(block, slot, slot + 1)
                backward(block, slot, slot + 1)

            @pl.when(jnp.logical_not(live))
            def _(slot=slot):
                y_ref[lat(block, slot)] = jnp.zeros((points, y_ref.shape[1]), BF)
                dz_ref[lat(block, slot)] = jnp.zeros((points, dz_ref.shape[1]), BF)

    most = largest(pc)
    pl.when(most <= LEAST)(lambda: body(LEAST))
    pl.when(most > LEAST)(lambda: body(USUAL))
    pl.when(most > USUAL)(lambda: lax.fori_loop(0, blocks, rest, None))
    split_slabs(total, own, mine, other)


def outer_kernel(pc, left_ref, right_ref, made_ref, out_ref, sent_ref):
    blocks = pc.shape[0]
    pairs = left_ref.shape[0] // blocks
    rows = pairs // SLOTS

    def body(used):
        if used == SLOTS:
            out_ref[...] = dot(right_ref[...], left_ref[...], ROWS_BY_ROWS)
            return
        for block in range(blocks):
            span = slice(block * pairs, block * pairs + used * rows)
            term = dot(right_ref[span], left_ref[span], ROWS_BY_ROWS)
            out_ref[...] = term if block == 0 else out_ref[...] + term

    by_count(pc, SLOTS, body)
    sent_ref[...] = made_ref[...].astype(BF)


def mesh_grad_kernel(s, t, w_own, w_other, out):
    half = out.shape[2]
    lift_own = (s[0].astype(FL) + t[1].astype(FL)).astype(BF)
    lift_other = (s[1].astype(FL) + t[0].astype(FL)).astype(BF)
    grad = dot(lift_own, w_own[...], COLS_BY_COLS) + dot(lift_other, w_other[...], COLS_BY_COLS)
    grad = grad.astype(BF)
    core = lax.axis_index("mp")

    @pl.when(core == 0)
    def _():
        out[0], out[1] = grad[:, :half], grad[:, half:]

    @pl.when(core == 1)
    def _():
        out[0], out[1] = grad[:, half:], grad[:, :half]


def encoder_grad_kernel(
    pm, pc, x_own, x_other, slope_ref, m, q1, q2, t1, t2, dec_ref, out_ref, near, total
):
    slots, blocks = pm.shape
    rows = near.shape[1]
    for at, ref in enumerate((m, q1, q2, t1, t2)):
        half = ref[0] if at < 3 else ref[...]
        near[at * OWNER_BLOCKS : (at + 1) * OWNER_BLOCKS] = half.reshape(OWNER_BLOCKS, rows, -1)

    def body(used):
        for first in range(0, blocks, 2):
            last = min(first + 2, blocks)
            parts = []
            for block in range(first, last):
                for slot in range(used):
                    picked = near[place(pm, block, slot, -1)].astype(FL)
                    start = (block * used + slot) * rows
                    parts.append((picked * slope_ref[start : start + rows].astype(FL)).astype(BF))
            du = jnp.concatenate(parts, axis=0)
            for at, x_ref in enumerate((x_own, x_other)):
                term = dot(du, x_ref[first * used * rows : last * used * rows], ROWS_BY_ROWS)
                total[at] = term if first == 0 else total[at] + term

    by_count(pc, slots, body)
    count, half = total.shape[1:]
    lanes = out_ref.shape[1]
    tiles = half // lanes

    def store(tile, value):
        out_ref[tile * count : (tile + 1) * count] = value.astype(BF)

    def store_encoder(order):
        for at, side in enumerate(order):
            for tile in range(tiles):
                store(at * tiles + tile, total[side, :, tile * lanes : (tile + 1) * lanes])

    core = lax.axis_index("mp")
    pl.when(core == 0)(lambda: store_encoder((0, 1)))
    pl.when(core == 1)(lambda: store_encoder((1, 0)))
    for tile in range(2 * tiles):
        store(2 * tiles + tile, dec_ref[:, tile * lanes : (tile + 1) * lanes])


def sum_kernel(parts_ref, out_ref):
    total = parts_ref[...].astype(FL).sum(axis=0).astype(BF)
    out_ref[...] = jnp.broadcast_to(total[None], out_ref.shape)


def finish_kernel(flat_ref, enc_ref, dec_ref):
    lanes = flat_ref.shape[1]
    width, count = enc_ref.shape
    for at, out in enumerate((enc_ref, dec_ref)):
        for tile in range(width // lanes):
            start = (at * width // lanes + tile) * count
            piece = flat_ref[start : start + count].astype(FL)
            out[tile * lanes : (tile + 1) * lanes] = piece.T


def plane_groups(count):
    across = min(16, count // 2)
    plane = [list(range(at, at + across)) for at in range(0, count, across)]
    line = [list(range(at, count, across)) for at in range(across)]
    return plane, line


def exchange(value, groups):
    return lax.all_to_all(value, "band", 0, 0, tiled=True, axis_index_groups=groups)


def params():
    return pltpu.CompilerParams(vmem_limit_bytes=24 * 2**20)


def shape_of(*shape, dtype=BF):
    return jax.ShapeDtypeStruct(shape, dtype)


def simple(kernel, out_shape):
    return pl.pallas_call(kernel, out_shape=out_shape, compiler_params=params())


def combine(own, parts):
    first, second = (part.astype(FL) for part in parts)
    total = first + second
    return jnp.stack([total[0] + own.astype(FL), total[1]]).astype(BF)


def reduce_to_owner(own, mine, other, beside=None):
    got = swap(other)
    parts = [outward(jnp.stack([mine[i], got[i]]), i + 1) for i in range(REACH)]
    parts, beside = lax.optimization_barrier((parts, beside))
    sums = combine(own, parts)
    return sums, swap(sums), beside


def spread_from_owner(value, wanted=lambda part: part):
    near = [outward(value, i + 1) for i in range(REACH)]
    swapped = [swap(wanted(near[0]))]
    for part in near[1:]:
        part, swapped[-1] = lax.optimization_barrier((part, swapped[-1]))
        swapped.append(swap(wanted(part)))
    return [value, *near, *swapped]


VMEM, HBM, SMEM = (pl.BlockSpec(memory_space=space) for space in (pltpu.VMEM, pltpu.HBM, pltpu.SMEM))


def held(kernel, in_specs, out_shape, scratch=(), cost=None):
    return pl.pallas_call(
        kernel,
        in_specs=in_specs,
        out_specs=jax.tree.map(lambda _: VMEM, out_shape),
        out_shape=out_shape,
        scratch_shapes=scratch,
        compiler_params=params(),
        cost_estimate=cost,
    )


def slab_shapes(owner_rows, half):
    return [shape_of(*lead, owner_rows, half) for lead in ((), (REACH,), (REACH,))]


def lift_own(*given):
    interp, grid, w_enc, pair_mesh, pair_count = given
    blocks, slots, rows, points = interp.shape
    half = w_enc.shape[1]
    pairs = blocks * slots * rows
    cost = pl.CostEstimate(flops=2 * pairs * points * half, bytes_accessed=4 * 2**20, transcendentals=0)
    fixed = [jax.ShapeDtypeStruct(value.shape, value.dtype) for value in (pair_mesh, pair_count)]
    return pl.pallas_call(
        lift_kernel,
        in_specs=[HBM] * 5,
        out_specs=[VMEM, VMEM, VMEM, SMEM, SMEM],
        out_shape=[shape_of(*interp.shape), shape_of(*w_enc.shape), shape_of(pairs, half), *fixed],
        scratch_shapes=[pltpu.VMEM(grid.shape, BF), pltpu.SemaphoreType.DMA((7,))],
        compiler_params=params(),
        cost_estimate=cost,
    )(*(pltpu.with_memory_space_constraint(value, pltpu.HBM) for value in given))


def encode(pair_mesh, pair_count, interp, w_enc, x_own, grid_other):
    blocks, slots, rows, points = interp.shape
    pairs, half = x_own.shape
    return held(
        encode_kernel,
        [SMEM, SMEM, *[VMEM] * 4],
        [shape_of(pairs, half), *slab_shapes(OWNER_BLOCKS * rows, half)],
        [pltpu.VMEM((NEAR * OWNER_BLOCKS, rows, half), FL)],
    )(pair_mesh, pair_count, interp, w_enc, x_own, grid_other)


def slopes(pair_count, w_enc, x_own, x_other):
    pairs, half = x_own.shape
    cost = pl.CostEstimate(
        flops=4 * pairs * half * half, bytes_accessed=6 * pairs * half, transcendentals=pairs * half
    )
    return held(slope_kernel, [SMEM, *[VMEM] * 3], shape_of(pairs, half), cost=cost)(
        pair_count, w_enc, x_own, x_other
    )


def decode(pair_mesh, pair_count, interp, grid, cotangent, w_dec, near):
    blocks, slots, rows, points = interp.shape
    full, half = w_dec.shape
    pairs = blocks * slots * points
    return held(
        decode_kernel,
        [SMEM, SMEM, *[VMEM] * (4 + NEAR)],
        [
            shape_of(*grid.shape, dtype=FL), shape_of(pairs, full), shape_of(pairs, half),
            *slab_shapes(OWNER_BLOCKS * rows, half),
        ],
        [
            pltpu.VMEM((NEAR * OWNER_BLOCKS, rows, full), BF),
            pltpu.VMEM((NEAR * OWNER_BLOCKS, rows, half), FL),
        ],
    )(pair_mesh, pair_count, interp, grid, cotangent, w_dec, *near)


def outer(pair_count, y, dz, made):
    pairs, full = y.shape
    half = dz.shape[1]
    cost = pl.CostEstimate(
        flops=2 * pairs * full * half, bytes_accessed=2 * pairs * (full + half), transcendentals=0
    )
    outs = [shape_of(half, full, dtype=FL), shape_of(*made.shape)]
    return held(outer_kernel, [SMEM, *[VMEM] * 3], outs, cost=cost)(pair_count, y, dz, made)


def encoder_grad(pair_mesh, pair_count, x_own, x_other, slope, near, grad_dec):
    half = slope.shape[1]
    rows = near[0].shape[1] // OWNER_BLOCKS
    return held(
        encoder_grad_kernel,
        [SMEM, SMEM, *[VMEM] * (4 + NEAR)],
        shape_of(8 * half, half // 2),
        [pltpu.VMEM((NEAR * OWNER_BLOCKS, rows, half), BF), pltpu.VMEM((2, half, half), FL)],
    )(pair_mesh, pair_count, x_own, x_other, slope, *near, grad_dec)


def local(grid, interp, mesh_init, w_enc, w_dec, cotangent, pair_mesh, pair_count):
    full, half = w_enc.shape
    pair_mesh = pair_mesh.T
    swapped = [swap(value) for value in (grid, mesh_init, w_dec)]
    grid_other, mesh_other, w_dec_other = lax.optimization_barrier(swapped)
    mesh_both = jnp.stack([mesh_init, mesh_other])

    interp, w_enc, x_own, pair_mesh, pair_count = lift_own(interp, grid, w_enc, pair_mesh, pair_count)
    x_other, own, mine, other = encode(pair_mesh, pair_count, interp, w_enc, x_own, grid_other)
    slope = slopes(pair_count, w_enc, x_own, x_other)
    sums, got, slope = reduce_to_owner(own, mine, other, slope)
    agg = sums.astype(FL) + got.astype(FL)[::-1]
    mesh_lat = (mesh_both.astype(FL) + 0.25 * agg).astype(BF)
    near = spread_from_owner(mesh_lat)

    out, y, dz, own, mine, other = decode(
        pair_mesh, pair_count, interp, grid, cotangent, w_dec, near
    )
    sums, got, (grad_dec, out) = reduce_to_owner(own, mine, other, outer(pair_count, y, dz, out))
    grad_mesh = simple(mesh_grad_kernel, shape_of(*sums.shape))(sums, got, w_dec, w_dec_other)
    near = spread_from_owner(grad_mesh, lambda part: part[1])
    flat = encoder_grad(pair_mesh, pair_count, x_own, x_other, slope, near, grad_dec)

    plane, line = plane_groups(lax.axis_size("band"))
    across = len(plane[0])
    chunks = exchange(flat.reshape(across, -1, half // 2), plane)
    piece = simple(sum_kernel, shape_of(len(line[0]), *chunks.shape[1:]))(chunks)
    pieces = exchange(piece, line)
    spread = simple(sum_kernel, shape_of(*chunks.shape))(pieces)
    flat = exchange(spread, plane).reshape(flat.shape)
    grads = [shape_of(full, half, dtype=FL)] * 2
    grad_enc, grad_dec = simple(finish_kernel, grads)(flat)
    return (out, grad_enc, grad_dec)


def solution(mesh):
    placed = (
        P("band", "mp"),
        P("band", None, None, None),
        P("band", "mp"),
        P(None, "mp"),
        P(None, "mp"),
        P("band", "mp"),
        P("band", None),
        P("band"),
    )
    return jax.shard_map(
        local,
        mesh=mesh,
        in_specs=placed,
        out_specs=(P("band", "mp"), P(None, "mp"), P(None, "mp")),
        check_vma=False,
    )
```

```python
import jax
import jax.numpy as jnp
from jax import lax
from jax.experimental import pallas as pl
from jax.experimental.pallas import tpu as pltpu
from jax.sharding import PartitionSpec as P

REACH = 2
NEAR = 2 * REACH + 1
OWNER_BLOCKS = 2
SLOTS = 4
LEAST, USUAL = 2, 3

FL, BF = jnp.float32, jnp.bfloat16
ROWS_BY_ROWS = (((0,), (0,)), ((), ()))
COLS_BY_COLS = (((1,), (1,)), ((), ()))


def dot(left, right, dims=(((1,), (0,)), ((), ()))):
    return lax.dot_general(left, right, dims, preferred_element_type=FL)


def swap(value):
    return lax.ppermute(value, "mp", [(0, 1), (1, 0)])


def outward(value, steps):
    count = lax.axis_size("band")
    pairs = []
    for band in range(count - steps):
        pairs.append((2 * band, 2 * (band + steps)))
        pairs.append((2 * (band + steps) + 1, 2 * band + 1))
    return lax.ppermute(value, ("band", "mp"), pairs)


def place(pm, block, slot, facing):
    target = pm[slot, block]
    offset = target // OWNER_BLOCKS - lax.axis_index("band")
    along = jnp.where(lax.axis_index("mp") == 0, offset, -offset) * facing
    along = jnp.clip(along, -REACH, REACH)
    stored = jnp.where(along >= 0, along, REACH - along)
    return stored * OWNER_BLOCKS + target % OWNER_BLOCKS


def live_of(pc, block, slot):
    return jnp.where(slot < pc[block], 1.0, 0.0).astype(FL)


def largest(pc):
    most = pc[0]
    for block in range(1, pc.shape[0]):
        most = jnp.maximum(most, pc[block])
    return most


def by_count(pc, slots, body):
    most = largest(pc)
    for used in range(LEAST, slots + 1):
        fits = most <= used if used == LEAST else (most >= used if used == slots else most == used)
        pl.when(fits)(lambda used=used: body(used))


def split_slabs(total, own, mine, other):
    blocks = own.shape[0] // total.shape[1]
    own[...] = total[:blocks].reshape(own.shape).astype(own.dtype)
    mine[...] = total[blocks : 3 * blocks].reshape(mine.shape).astype(mine.dtype)
    other[...] = total[3 * blocks :].reshape(other.shape).astype(other.dtype)


def sigmoid(value):
    return 0.5 * jnp.tanh(0.5 * value) + 0.5


def fetch(pairs, sems):
    copies = [pltpu.make_async_copy(src, dst, sems.at[at]) for at, (src, dst) in enumerate(pairs)]
    for copy in copies:
        copy.start()
    return copies


def lift_kernel(a_hbm, g_hbm, w_hbm, pm_hbm, pc_hbm, a_ref, w_ref, x_ref, pm_ref, pc_ref, g_ref, sems):
    blocks, slots, rows, points = a_ref.shape
    pairs = slots * rows
    early = 2
    parts = []
    for start, size in ((0, early), (early, blocks - early)):
        points_at, blocks_at = pl.ds(start * points, size * points), pl.ds(start, size)
        parts.append((g_hbm.at[points_at], g_ref.at[points_at]))
        parts.append((a_hbm.at[blocks_at], a_ref.at[blocks_at]))
    copies = fetch([*parts, (w_hbm, w_ref), (pm_hbm, pm_ref), (pc_hbm, pc_ref)], sems)
    copies[-1].wait()
    for copy in copies[:2]:
        copy.wait()

    def body(used):
        for block in range(blocks):
            if block == early:
                for copy in copies[2:4]:
                    copy.wait()
            weights = a_ref[block, :used].reshape(used * rows, points)
            x = dot(weights, g_ref[block * points : (block + 1) * points])
            x_ref[block * used * rows : (block + 1) * used * rows] = x.astype(BF)

    by_count(pc_ref, slots, body)
    for copy in copies[4:-1]:
        copy.wait()


def by_side(w_ref):
    half = w_ref.shape[0] // 2
    core = lax.axis_index("mp")
    return [w_ref[pl.ds(pl.multiple_of(side * half, half), half)] for side in (core, 1 - core)]


def encode_kernel(
    pm, pc, a_ref, w_ref, x_own, g_other, x_other, own, mine, other, total
):
    blocks, slots, rows, points = a_ref.shape
    pairs = slots * rows
    total[...] = jnp.zeros_like(total)

    def body(used):
        w_own, w_far = by_side(w_ref)
        for block in range(blocks):
            span = slice(block * used * rows, (block + 1) * used * rows)
            weights = a_ref[block, :used].reshape(used * rows, points)
            x = dot(weights, g_other[block * points : (block + 1) * points]).astype(BF)
            x_other[span] = x
            u = dot(x_own[span], w_own) + dot(x, w_far)
            for slot in range(used):
                part = u[slot * rows : (slot + 1) * rows]
                sig = sigmoid(part)
                total[place(pm, block, slot, 1)] += part * sig * live_of(pc, block, slot)

    by_count(pc, slots, body)
    split_slabs(total, own, mine, other)


def slope_kernel(pc, w_ref, x_own, x_other, slope_ref):
    blocks = pc.shape[0]
    pairs = x_own.shape[0] // blocks
    rows = pairs // SLOTS

    def body(used):
        w_own, w_far = by_side(w_ref)
        for block in range(blocks):
            span = slice(block * used * rows, (block + 1) * used * rows)
            u = dot(x_own[span], w_own) + dot(x_other[span], w_far)
            for slot in range(used):
                part = u[slot * rows : (slot + 1) * rows]
                sig = sigmoid(part)
                slope = (sig + part * sig * (1.0 - sig)) * (0.25 * live_of(pc, block, slot))
                at = (block * used + slot) * rows
                slope_ref[at : at + rows] = slope.astype(BF)

    by_count(pc, SLOTS, body)


def gather_near(near, refs, picks):
    blocks = near.shape[0] // len(refs)
    rows, width = near.shape[1], near.shape[2] // 2

    def fill(own_at):
        for at, (ref, pick) in enumerate(zip(refs, picks)):
            for half in range(2):
                column = (own_at + half) % 2 * width
                value = ref[half ^ pick].reshape(blocks, rows, width)
                near[at * blocks : (at + 1) * blocks, :, column : column + width] = value

    core = lax.axis_index("mp")
    pl.when(core == 0)(lambda: fill(0))
    pl.when(core == 1)(lambda: fill(1))


def decode_kernel(
    pm, pc, a_ref, g_ref, cot_ref, w_ref, m, q1, q2, t1, t2,
    out_ref, y_ref, dz_ref, own, mine, other, near, total,
):
    blocks, slots, rows, points = a_ref.shape
    pairs = slots * points
    total[...] = jnp.zeros_like(total)
    gather_near(near, (m, q1, q2, t1, t2), (0, 0, 0, 1, 1))

    def lat(block, slot):
        at = block * pairs + slot * points
        return pl.ds(at if isinstance(block, int) else pl.multiple_of(at, points), points)

    def points_of(block):
        at = block * points
        return pl.ds(at if isinstance(block, int) else pl.multiple_of(at, points), points)

    def forward(block, first, last):
        for slot in range(first, last):
            chosen = near[place(pm, block, slot, -1)]
            y_ref[lat(block, slot)] = dot(a_ref[block, slot], chosen, ROWS_BY_ROWS).astype(BF)
        span = points_of(block)
        z = dot(y_ref[pl.ds(lat(block, first).start, (last - first) * points)], w_ref[...])
        result = (out_ref[span] if first else g_ref[span]).astype(FL)
        upstream = cot_ref[span].astype(FL)
        for slot in range(first, last):
            part = z[(slot - first) * points : (slot - first + 1) * points]
            sig = sigmoid(part)
            edge = part * sig
            live = live_of(pc, block, slot)
            result = result + edge * live
            slope = sig + edge * (1.0 - sig)
            dz_ref[lat(block, slot)] = ((upstream * live) * slope).astype(BF)
        out_ref[span] = result

    def backward(block, first, last):
        for slot in range(first, last):
            lift = dot(a_ref[block, slot], dz_ref[lat(block, slot)])
            total[place(pm, block, slot, 1)] += lift

    def body(used):
        for step in (forward, backward):
            for block in range(blocks):
                step(block, 0, used)

    def rest(block, _):
        for slot in range(USUAL, slots):
            live = slot < pc[block]

            @pl.when(live)
            def _(slot=slot):
                forward(block, slot, slot + 1)
                backward(block, slot, slot + 1)

            @pl.when(jnp.logical_not(live))
            def _(slot=slot):
                y_ref[lat(block, slot)] = jnp.zeros((points, y_ref.shape[1]), BF)
                dz_ref[lat(block, slot)] = jnp.zeros((points, dz_ref.shape[1]), BF)

    most = largest(pc)
    pl.when(most <= LEAST)(lambda: body(LEAST))
    pl.when(most > LEAST)(lambda: body(USUAL))
    pl.when(most > USUAL)(lambda: lax.fori_loop(0, blocks, rest, None))
    split_slabs(total, own, mine, other)


def outer_kernel(pc, left_ref, right_ref, made_ref, out_ref, sent_ref):
    blocks = pc.shape[0]
    pairs = left_ref.shape[0] // blocks
    rows = pairs // SLOTS

    def body(used):
        if used == SLOTS:
            out_ref[...] = dot(right_ref[...], left_ref[...], ROWS_BY_ROWS)
            return
        for block in range(blocks):
            span = slice(block * pairs, block * pairs + used * rows)
            term = dot(right_ref[span], left_ref[span], ROWS_BY_ROWS)
            out_ref[...] = term if block == 0 else out_ref[...] + term

    by_count(pc, SLOTS, body)
    sent_ref[...] = made_ref[...].astype(BF)


def mesh_grad_kernel(s, t, w_own, w_other, out):
    half = out.shape[2]
    lift_own = (s[0].astype(FL) + t[1].astype(FL)).astype(BF)
    lift_other = (s[1].astype(FL) + t[0].astype(FL)).astype(BF)
    grad = dot(lift_own, w_own[...], COLS_BY_COLS) + dot(lift_other, w_other[...], COLS_BY_COLS)
    grad = grad.astype(BF)
    core = lax.axis_index("mp")

    @pl.when(core == 0)
    def _():
        out[0], out[1] = grad[:, :half], grad[:, half:]

    @pl.when(core == 1)
    def _():
        out[0], out[1] = grad[:, half:], grad[:, :half]


def encoder_grad_kernel(
    pm, pc, x_own, x_other, slope_ref, m, q1, q2, t1, t2, dec_ref, out_ref, near, total
):
    slots, blocks = pm.shape
    rows = near.shape[1]
    for at, ref in enumerate((m, q1, q2, t1, t2)):
        half = ref[0] if at < 3 else ref[...]
        near[at * OWNER_BLOCKS : (at + 1) * OWNER_BLOCKS] = half.reshape(OWNER_BLOCKS, rows, -1)

    def body(used):
        for first in range(0, blocks, 2):
            last = min(first + 2, blocks)
            parts = []
            for block in range(first, last):
                for slot in range(used):
                    picked = near[place(pm, block, slot, -1)].astype(FL)
                    start = (block * used + slot) * rows
                    parts.append((picked * slope_ref[start : start + rows].astype(FL)).astype(BF))
            du = jnp.concatenate(parts, axis=0)
            for at, x_ref in enumerate((x_own, x_other)):
                term = dot(du, x_ref[first * used * rows : last * used * rows], ROWS_BY_ROWS)
                total[at] = term if first == 0 else total[at] + term

    by_count(pc, slots, body)
    count, half = total.shape[1:]
    lanes = out_ref.shape[1]
    tiles = half // lanes

    def store(tile, value):
        out_ref[tile * count : (tile + 1) * count] = value.astype(BF)

    def store_encoder(order):
        for at, side in enumerate(order):
            for tile in range(tiles):
                store(at * tiles + tile, total[side, :, tile * lanes : (tile + 1) * lanes])

    core = lax.axis_index("mp")
    pl.when(core == 0)(lambda: store_encoder((0, 1)))
    pl.when(core == 1)(lambda: store_encoder((1, 0)))
    for tile in range(2 * tiles):
        store(2 * tiles + tile, dec_ref[:, tile * lanes : (tile + 1) * lanes])


def sum_kernel(parts_ref, out_ref):
    total = parts_ref[...].astype(FL).sum(axis=0).astype(BF)
    out_ref[...] = jnp.broadcast_to(total[None], out_ref.shape)


def finish_kernel(flat_ref, enc_ref, dec_ref):
    lanes = flat_ref.shape[1]
    width, count = enc_ref.shape
    for at, out in enumerate((enc_ref, dec_ref)):
        for tile in range(width // lanes):
            start = (at * width // lanes + tile) * count
            piece = flat_ref[start : start + count].astype(FL)
            out[tile * lanes : (tile + 1) * lanes] = piece.T


def plane_groups(count):
    across = min(16, count // 2)
    plane = [list(range(at, at + across)) for at in range(0, count, across)]
    line = [list(range(at, count, across)) for at in range(across)]
    return plane, line


def exchange(value, groups):
    return lax.all_to_all(value, "band", 0, 0, tiled=True, axis_index_groups=groups)


def params():
    return pltpu.CompilerParams(vmem_limit_bytes=24 * 2**20)


def shape_of(*shape, dtype=BF):
    return jax.ShapeDtypeStruct(shape, dtype)


def simple(kernel, out_shape):
    return pl.pallas_call(kernel, out_shape=out_shape, compiler_params=params())


def combine(own, parts):
    near, far = parts
    near = near.astype(FL)
    base = jnp.stack([near[0] + own.astype(FL), near[1]])
    base, far = lax.optimization_barrier((base, far))
    return (base + far.astype(FL)).astype(BF)


def reduce_to_owner(own, mine, other, beside=None):
    got = swap(other)
    parts = [outward(jnp.stack([mine[i], got[i]]), i + 1) for i in range(REACH)]
    parts[1], beside = lax.optimization_barrier((parts[1], beside))
    sums = combine(own, parts)
    return sums, swap(sums), beside


def spread_from_owner(value, wanted=lambda part: part):
    near = [outward(value, i + 1) for i in range(REACH)]
    return [value, *near, *(swap(wanted(part)) for part in near)]


VMEM, HBM, SMEM = (pl.BlockSpec(memory_space=space) for space in (pltpu.VMEM, pltpu.HBM, pltpu.SMEM))


def held(kernel, in_specs, out_shape, scratch=(), cost=None):
    return pl.pallas_call(
        kernel,
        in_specs=in_specs,
        out_specs=jax.tree.map(lambda _: VMEM, out_shape),
        out_shape=out_shape,
        scratch_shapes=scratch,
        compiler_params=params(),
        cost_estimate=cost,
    )


def slab_shapes(owner_rows, half):
    return [shape_of(*lead, owner_rows, half) for lead in ((), (REACH,), (REACH,))]


def lift_own(*given):
    interp, grid, w_enc, pair_mesh, pair_count = given
    blocks, slots, rows, points = interp.shape
    half = w_enc.shape[1]
    pairs = blocks * slots * rows
    cost = pl.CostEstimate(flops=2 * pairs * points * half, bytes_accessed=4 * 2**20, transcendentals=0)
    fixed = [jax.ShapeDtypeStruct(value.shape, value.dtype) for value in (pair_mesh, pair_count)]
    return pl.pallas_call(
        lift_kernel,
        in_specs=[HBM] * 5,
        out_specs=[VMEM, VMEM, VMEM, SMEM, SMEM],
        out_shape=[shape_of(*interp.shape), shape_of(*w_enc.shape), shape_of(pairs, half), *fixed],
        scratch_shapes=[pltpu.VMEM(grid.shape, BF), pltpu.SemaphoreType.DMA((7,))],
        compiler_params=params(),
        cost_estimate=cost,
    )(*(pltpu.with_memory_space_constraint(value, pltpu.HBM) for value in given))


def encode(pair_mesh, pair_count, interp, w_enc, x_own, grid_other):
    blocks, slots, rows, points = interp.shape
    pairs, half = x_own.shape
    return held(
        encode_kernel,
        [SMEM, SMEM, *[VMEM] * 4],
        [shape_of(pairs, half), *slab_shapes(OWNER_BLOCKS * rows, half)],
        [pltpu.VMEM((NEAR * OWNER_BLOCKS, rows, half), FL)],
    )(pair_mesh, pair_count, interp, w_enc, x_own, grid_other)


def slopes(pair_count, w_enc, x_own, x_other):
    pairs, half = x_own.shape
    cost = pl.CostEstimate(
        flops=4 * pairs * half * half, bytes_accessed=6 * pairs * half, transcendentals=pairs * half
    )
    return held(slope_kernel, [SMEM, *[VMEM] * 3], shape_of(pairs, half), cost=cost)(
        pair_count, w_enc, x_own, x_other
    )


def decode(pair_mesh, pair_count, interp, grid, cotangent, w_dec, near):
    blocks, slots, rows, points = interp.shape
    full, half = w_dec.shape
    pairs = blocks * slots * points
    return held(
        decode_kernel,
        [SMEM, SMEM, *[VMEM] * (4 + NEAR)],
        [
            shape_of(*grid.shape, dtype=FL), shape_of(pairs, full), shape_of(pairs, half),
            *slab_shapes(OWNER_BLOCKS * rows, half),
        ],
        [
            pltpu.VMEM((NEAR * OWNER_BLOCKS, rows, full), BF),
            pltpu.VMEM((NEAR * OWNER_BLOCKS, rows, half), FL),
        ],
    )(pair_mesh, pair_count, interp, grid, cotangent, w_dec, *near)


def outer(pair_count, y, dz, made):
    pairs, full = y.shape
    half = dz.shape[1]
    cost = pl.CostEstimate(
        flops=2 * pairs * full * half, bytes_accessed=2 * pairs * (full + half), transcendentals=0
    )
    outs = [shape_of(half, full, dtype=FL), shape_of(*made.shape)]
    return held(outer_kernel, [SMEM, *[VMEM] * 3], outs, cost=cost)(pair_count, y, dz, made)


def encoder_grad(pair_mesh, pair_count, x_own, x_other, slope, near, grad_dec):
    half = slope.shape[1]
    rows = near[0].shape[1] // OWNER_BLOCKS
    return held(
        encoder_grad_kernel,
        [SMEM, SMEM, *[VMEM] * (4 + NEAR)],
        shape_of(8 * half, half // 2),
        [pltpu.VMEM((NEAR * OWNER_BLOCKS, rows, half), BF), pltpu.VMEM((2, half, half), FL)],
    )(pair_mesh, pair_count, x_own, x_other, slope, *near, grad_dec)


def local(grid, interp, mesh_init, w_enc, w_dec, cotangent, pair_mesh, pair_count):
    full, half = w_enc.shape
    pair_mesh = pair_mesh.T
    swapped = [swap(value) for value in (grid, mesh_init, w_dec)]
    grid_other, mesh_other, w_dec_other = lax.optimization_barrier(swapped)
    mesh_both = jnp.stack([mesh_init, mesh_other])

    interp, w_enc, x_own, pair_mesh, pair_count = lift_own(interp, grid, w_enc, pair_mesh, pair_count)
    x_other, own, mine, other = encode(pair_mesh, pair_count, interp, w_enc, x_own, grid_other)
    slope = slopes(pair_count, w_enc, x_own, x_other)
    sums, got, slope = reduce_to_owner(own, mine, other, slope)
    agg = sums.astype(FL) + got.astype(FL)[::-1]
    mesh_lat = (mesh_both.astype(FL) + 0.25 * agg).astype(BF)
    near = spread_from_owner(mesh_lat)

    out, y, dz, own, mine, other = decode(
        pair_mesh, pair_count, interp, grid, cotangent, w_dec, near
    )
    sums, got, (grad_dec, out) = reduce_to_owner(own, mine, other, outer(pair_count, y, dz, out))
    grad_mesh = simple(mesh_grad_kernel, shape_of(*sums.shape))(sums, got, w_dec, w_dec_other)
    near = spread_from_owner(grad_mesh, lambda part: part[1])
    flat = encoder_grad(pair_mesh, pair_count, x_own, x_other, slope, near, grad_dec)

    plane, line = plane_groups(lax.axis_size("band"))
    across = len(plane[0])
    chunks = exchange(flat.reshape(across, -1, half // 2), plane)
    piece = simple(sum_kernel, shape_of(len(line[0]), *chunks.shape[1:]))(chunks)
    pieces = exchange(piece, line)
    spread = simple(sum_kernel, shape_of(*chunks.shape))(pieces)
    flat = exchange(spread, plane).reshape(flat.shape)
    grads = [shape_of(full, half, dtype=FL)] * 2
    grad_enc, grad_dec = simple(finish_kernel, grads)(flat)
    return (out, grad_enc, grad_dec)


def solution(mesh):
    placed = (
        P("band", "mp"),
        P("band", None, None, None),
        P("band", "mp"),
        P(None, "mp"),
        P(None, "mp"),
        P("band", "mp"),
        P("band", None),
        P("band"),
    )
    return jax.shard_map(
        local,
        mesh=mesh,
        in_specs=placed,
        out_specs=(P("band", "mp"), P(None, "mp"), P(None, "mp")),
        check_vma=False,
    )
```

```python
import jax
import jax.numpy as jnp
from jax import lax
from jax.experimental import pallas as pl
from jax.experimental.pallas import tpu as pltpu
from jax.sharding import PartitionSpec as P

REACH = 2
NEAR = 2 * REACH + 1
OWNER_BLOCKS = 2
SLOTS = 4
LEAST, USUAL = 2, 3

FL, BF = jnp.float32, jnp.bfloat16
ROWS_BY_ROWS = (((0,), (0,)), ((), ()))
COLS_BY_COLS = (((1,), (1,)), ((), ()))


def dot(left, right, dims=(((1,), (0,)), ((), ()))):
    return lax.dot_general(left, right, dims, preferred_element_type=FL)


def swap(value):
    return lax.ppermute(value, "mp", [(0, 1), (1, 0)])


def outward(value, steps):
    count = lax.axis_size("band")
    pairs = []
    for band in range(count - steps):
        low, high = 2 * band, 2 * (band + steps) + 1
        pairs += [(low, high), (high, low)]
    return lax.ppermute(value, ("band", "mp"), pairs)


def place(pm, block, slot):
    target = pm[slot, block]
    offset = target // OWNER_BLOCKS - lax.axis_index("band")
    along = jnp.where(lax.axis_index("mp") == 0, offset, -offset)
    along = jnp.clip(along, -REACH, REACH)
    stored = jnp.where(along >= 0, along, REACH - along)
    return stored * OWNER_BLOCKS + target % OWNER_BLOCKS


def live_of(pc, block, slot):
    return jnp.where(slot < pc[block], 1.0, 0.0).astype(FL)


def largest(pc):
    most = pc[0]
    for block in range(1, pc.shape[0]):
        most = jnp.maximum(most, pc[block])
    return most


def by_count(pc, slots, body):
    most = largest(pc)
    for used in range(LEAST, slots + 1):
        fits = most <= used if used == LEAST else (most >= used if used == slots else most == used)
        pl.when(fits)(lambda used=used: body(used))


def split_slabs(total, own, mine, other):
    blocks = own.shape[0] // total.shape[1]
    own[...] = total[:blocks].reshape(own.shape).astype(own.dtype)
    mine[...] = total[blocks : 3 * blocks].reshape(mine.shape).astype(mine.dtype)
    other[...] = total[3 * blocks :].reshape(other.shape).astype(other.dtype)


def sigmoid(value):
    return 0.5 * jnp.tanh(0.5 * value) + 0.5


def fetch(pairs, sems):
    copies = [pltpu.make_async_copy(src, dst, sems.at[at]) for at, (src, dst) in enumerate(pairs)]
    for copy in copies:
        copy.start()
    return copies


def lift_kernel(a_hbm, g_hbm, w_hbm, pm_hbm, pc_hbm, a_ref, w_ref, x_ref, pm_ref, pc_ref, g_ref, sems):
    blocks, slots, rows, points = a_ref.shape
    pairs = slots * rows
    early = 2
    parts = []
    for start, size in ((0, early), (early, blocks - early)):
        points_at, blocks_at = pl.ds(start * points, size * points), pl.ds(start, size)
        parts.append((g_hbm.at[points_at], g_ref.at[points_at]))
        parts.append((a_hbm.at[blocks_at], a_ref.at[blocks_at]))
    copies = fetch([*parts, (w_hbm, w_ref), (pm_hbm, pm_ref), (pc_hbm, pc_ref)], sems)
    copies[-1].wait()
    for copy in copies[:2]:
        copy.wait()

    def body(used):
        for block in range(blocks):
            if block == early:
                for copy in copies[2:4]:
                    copy.wait()
            weights = a_ref[block, :used].reshape(used * rows, points)
            x = dot(weights, g_ref[block * points : (block + 1) * points])
            x_ref[block * used * rows : (block + 1) * used * rows] = x.astype(BF)

    by_count(pc_ref, slots, body)
    for copy in copies[4:-1]:
        copy.wait()


def by_side(w_ref):
    half = w_ref.shape[0] // 2
    core = lax.axis_index("mp")
    return [w_ref[pl.ds(pl.multiple_of(side * half, half), half)] for side in (core, 1 - core)]


def encode_kernel(
    pm, pc, a_ref, w_ref, x_own, g_other, x_other, own, mine, other, total
):
    blocks, slots, rows, points = a_ref.shape
    pairs = slots * rows
    total[...] = jnp.zeros_like(total)

    def body(used):
        w_own, w_far = by_side(w_ref)
        for block in range(blocks):
            span = slice(block * used * rows, (block + 1) * used * rows)
            weights = a_ref[block, :used].reshape(used * rows, points)
            x = dot(weights, g_other[block * points : (block + 1) * points]).astype(BF)
            x_other[span] = x
            u = dot(x_own[span], w_own) + dot(x, w_far)
            for slot in range(used):
                part = u[slot * rows : (slot + 1) * rows]
                sig = sigmoid(part)
                total[place(pm, block, slot)] += part * sig * live_of(pc, block, slot)

    by_count(pc, slots, body)
    split_slabs(total, own, mine, other)


def slope_kernel(pc, w_ref, x_own, x_other, slope_ref):
    blocks = pc.shape[0]
    pairs = x_own.shape[0] // blocks
    rows = pairs // SLOTS

    def body(used):
        w_own, w_far = by_side(w_ref)
        for block in range(blocks):
            span = slice(block * used * rows, (block + 1) * used * rows)
            u = dot(x_own[span], w_own) + dot(x_other[span], w_far)
            for slot in range(used):
                part = u[slot * rows : (slot + 1) * rows]
                sig = sigmoid(part)
                slope = (sig + part * sig * (1.0 - sig)) * (0.25 * live_of(pc, block, slot))
                at = (block * used + slot) * rows
                slope_ref[at : at + rows] = slope.astype(BF)

    by_count(pc, SLOTS, body)


def gather_near(near, refs, picks):
    blocks = near.shape[0] // len(refs)
    rows, width = near.shape[1], near.shape[2] // 2

    def fill(own_at):
        for at, (ref, pick) in enumerate(zip(refs, picks)):
            for half in range(2):
                column = (own_at + half) % 2 * width
                value = ref[half ^ pick].reshape(blocks, rows, width)
                near[at * blocks : (at + 1) * blocks, :, column : column + width] = value

    core = lax.axis_index("mp")
    pl.when(core == 0)(lambda: fill(0))
    pl.when(core == 1)(lambda: fill(1))


def decode_kernel(
    pm, pc, a_ref, g_ref, cot_ref, w_ref, m, q1, q2, t1, t2,
    out_ref, y_ref, dz_ref, own, mine, other, near, total,
):
    blocks, slots, rows, points = a_ref.shape
    pairs = slots * points
    total[...] = jnp.zeros_like(total)
    gather_near(near, (m, q1, q2, t1, t2), (0, 1, 1, 0, 0))

    def lat(block, slot):
        at = block * pairs + slot * points
        return pl.ds(at if isinstance(block, int) else pl.multiple_of(at, points), points)

    def points_of(block):
        at = block * points
        return pl.ds(at if isinstance(block, int) else pl.multiple_of(at, points), points)

    def forward(block, first, last):
        for slot in range(first, last):
            chosen = near[place(pm, block, slot)]
            y_ref[lat(block, slot)] = dot(a_ref[block, slot], chosen, ROWS_BY_ROWS).astype(BF)
        span = points_of(block)
        z = dot(y_ref[pl.ds(lat(block, first).start, (last - first) * points)], w_ref[...])
        result = (out_ref[span] if first else g_ref[span]).astype(FL)
        upstream = cot_ref[span].astype(FL)
        for slot in range(first, last):
            part = z[(slot - first) * points : (slot - first + 1) * points]
            sig = sigmoid(part)
            edge = part * sig
            live = live_of(pc, block, slot)
            result = result + edge * live
            slope = sig + edge * (1.0 - sig)
            dz_ref[lat(block, slot)] = ((upstream * live) * slope).astype(BF)
        out_ref[span] = result

    def backward(block, first, last):
        for slot in range(first, last):
            lift = dot(a_ref[block, slot], dz_ref[lat(block, slot)])
            total[place(pm, block, slot)] += lift

    def body(used):
        for step in (forward, backward):
            for block in range(blocks):
                step(block, 0, used)

    def rest(block, _):
        for slot in range(USUAL, slots):
            live = slot < pc[block]

            @pl.when(live)
            def _(slot=slot):
                forward(block, slot, slot + 1)
                backward(block, slot, slot + 1)

            @pl.when(jnp.logical_not(live))
            def _(slot=slot):
                y_ref[lat(block, slot)] = jnp.zeros((points, y_ref.shape[1]), BF)
                dz_ref[lat(block, slot)] = jnp.zeros((points, dz_ref.shape[1]), BF)

    most = largest(pc)
    pl.when(most <= LEAST)(lambda: body(LEAST))
    pl.when(most > LEAST)(lambda: body(USUAL))
    pl.when(most > USUAL)(lambda: lax.fori_loop(0, blocks, rest, None))
    split_slabs(total, own, mine, other)


def outer_kernel(pc, left_ref, right_ref, made_ref, out_ref, sent_ref):
    blocks = pc.shape[0]
    pairs = left_ref.shape[0] // blocks
    rows = pairs // SLOTS

    def body(used):
        if used == SLOTS:
            out_ref[...] = dot(right_ref[...], left_ref[...], ROWS_BY_ROWS)
            return
        for block in range(blocks):
            span = slice(block * pairs, block * pairs + used * rows)
            term = dot(right_ref[span], left_ref[span], ROWS_BY_ROWS)
            out_ref[...] = term if block == 0 else out_ref[...] + term

    by_count(pc, SLOTS, body)
    sent_ref[...] = made_ref[...].astype(BF)


def mesh_grad_kernel(s, t, w_own, w_other, out):
    half = out.shape[2]
    lift_own = (s[0].astype(FL) + t[1].astype(FL)).astype(BF)
    lift_other = (s[1].astype(FL) + t[0].astype(FL)).astype(BF)
    grad = dot(lift_own, w_own[...], COLS_BY_COLS) + dot(lift_other, w_other[...], COLS_BY_COLS)
    grad = grad.astype(BF)
    core = lax.axis_index("mp")

    @pl.when(core == 0)
    def _():
        out[0], out[1] = grad[:, :half], grad[:, half:]

    @pl.when(core == 1)
    def _():
        out[0], out[1] = grad[:, half:], grad[:, :half]


def encoder_grad_kernel(
    pm, pc, x_own, x_other, slope_ref, m, q1, q2, t1, t2, dec_ref, out_ref, near, total
):
    slots, blocks = pm.shape
    rows = near.shape[1]
    for at, ref in enumerate((m, q1, q2, t1, t2)):
        half = ref[...] if at > REACH else ref[min(at, 1)]
        near[at * OWNER_BLOCKS : (at + 1) * OWNER_BLOCKS] = half.reshape(OWNER_BLOCKS, rows, -1)

    def body(used):
        for first in range(0, blocks, 2):
            last = min(first + 2, blocks)
            parts = []
            for block in range(first, last):
                for slot in range(used):
                    picked = near[place(pm, block, slot)].astype(FL)
                    start = (block * used + slot) * rows
                    parts.append((picked * slope_ref[start : start + rows].astype(FL)).astype(BF))
            du = jnp.concatenate(parts, axis=0)
            for at, x_ref in enumerate((x_own, x_other)):
                term = dot(du, x_ref[first * used * rows : last * used * rows], ROWS_BY_ROWS)
                total[at] = term if first == 0 else total[at] + term

    by_count(pc, slots, body)
    count, half = total.shape[1:]
    lanes = out_ref.shape[1]
    tiles = half // lanes

    def store(tile, value):
        out_ref[tile * count : (tile + 1) * count] = value.astype(BF)

    def store_encoder(order):
        for at, side in enumerate(order):
            for tile in range(tiles):
                store(at * tiles + tile, total[side, :, tile * lanes : (tile + 1) * lanes])

    core = lax.axis_index("mp")
    pl.when(core == 0)(lambda: store_encoder((0, 1)))
    pl.when(core == 1)(lambda: store_encoder((1, 0)))
    for tile in range(2 * tiles):
        store(2 * tiles + tile, dec_ref[:, tile * lanes : (tile + 1) * lanes])


def sum_kernel(parts_ref, out_ref):
    total = parts_ref[...].astype(FL).sum(axis=0).astype(BF)
    out_ref[...] = jnp.broadcast_to(total[None], out_ref.shape)


def finish_kernel(flat_ref, enc_ref, dec_ref):
    lanes = flat_ref.shape[1]
    width, count = enc_ref.shape
    for at, out in enumerate((enc_ref, dec_ref)):
        for tile in range(width // lanes):
            start = (at * width // lanes + tile) * count
            piece = flat_ref[start : start + count].astype(FL)
            out[tile * lanes : (tile + 1) * lanes] = piece.T


def plane_groups(count):
    across = min(16, count // 2)
    plane = [list(range(at, at + across)) for at in range(0, count, across)]
    line = [list(range(at, count, across)) for at in range(across)]
    return plane, line


def exchange(value, groups):
    return lax.all_to_all(value, "band", 0, 0, tiled=True, axis_index_groups=groups)


def params():
    return pltpu.CompilerParams(vmem_limit_bytes=24 * 2**20)


def shape_of(*shape, dtype=BF):
    return jax.ShapeDtypeStruct(shape, dtype)


def simple(kernel, out_shape):
    return pl.pallas_call(kernel, out_shape=out_shape, compiler_params=params())


def combine(own, parts):
    near, far = parts
    near = near.astype(FL)
    base = jnp.stack([near[1] + own.astype(FL), near[0]])
    base, far = lax.optimization_barrier((base, far))
    return (base + far.astype(FL)[::-1]).astype(BF)


def reduce_to_owner(own, mine, other, beside=None):
    got = swap(other)
    parts = [outward(jnp.stack([mine[i], got[i]]), i + 1) for i in range(REACH)]
    parts[1], beside = lax.optimization_barrier((parts[1], beside))
    sums = combine(own, parts)
    return sums, swap(sums), beside


def spread_from_owner(value, wanted=lambda part: part):
    near = [outward(value, i + 1) for i in range(REACH)]
    return [value, *near, *(swap(wanted(part)) for part in near)]


VMEM, HBM, SMEM = (pl.BlockSpec(memory_space=space) for space in (pltpu.VMEM, pltpu.HBM, pltpu.SMEM))


def held(kernel, in_specs, out_shape, scratch=(), cost=None):
    return pl.pallas_call(
        kernel,
        in_specs=in_specs,
        out_specs=jax.tree.map(lambda _: VMEM, out_shape),
        out_shape=out_shape,
        scratch_shapes=scratch,
        compiler_params=params(),
        cost_estimate=cost,
    )


def slab_shapes(owner_rows, half):
    return [shape_of(*lead, owner_rows, half) for lead in ((), (REACH,), (REACH,))]


def lift_own(*given):
    interp, grid, w_enc, pair_mesh, pair_count = given
    blocks, slots, rows, points = interp.shape
    half = w_enc.shape[1]
    pairs = blocks * slots * rows
    cost = pl.CostEstimate(flops=2 * pairs * points * half, bytes_accessed=4 * 2**20, transcendentals=0)
    fixed = [jax.ShapeDtypeStruct(value.shape, value.dtype) for value in (pair_mesh, pair_count)]
    return pl.pallas_call(
        lift_kernel,
        in_specs=[HBM] * 5,
        out_specs=[VMEM, VMEM, VMEM, SMEM, SMEM],
        out_shape=[shape_of(*interp.shape), shape_of(*w_enc.shape), shape_of(pairs, half), *fixed],
        scratch_shapes=[pltpu.VMEM(grid.shape, BF), pltpu.SemaphoreType.DMA((7,))],
        compiler_params=params(),
        cost_estimate=cost,
    )(*(pltpu.with_memory_space_constraint(value, pltpu.HBM) for value in given))


def encode(pair_mesh, pair_count, interp, w_enc, x_own, grid_other):
    blocks, slots, rows, points = interp.shape
    pairs, half = x_own.shape
    return held(
        encode_kernel,
        [SMEM, SMEM, *[VMEM] * 4],
        [shape_of(pairs, half), *slab_shapes(OWNER_BLOCKS * rows, half)],
        [pltpu.VMEM((NEAR * OWNER_BLOCKS, rows, half), FL)],
    )(pair_mesh, pair_count, interp, w_enc, x_own, grid_other)


def slopes(pair_count, w_enc, x_own, x_other):
    pairs, half = x_own.shape
    cost = pl.CostEstimate(
        flops=4 * pairs * half * half, bytes_accessed=6 * pairs * half, transcendentals=pairs * half
    )
    return held(slope_kernel, [SMEM, *[VMEM] * 3], shape_of(pairs, half), cost=cost)(
        pair_count, w_enc, x_own, x_other
    )


def decode(pair_mesh, pair_count, interp, grid, cotangent, w_dec, near):
    blocks, slots, rows, points = interp.shape
    full, half = w_dec.shape
    pairs = blocks * slots * points
    return held(
        decode_kernel,
        [SMEM, SMEM, *[VMEM] * (4 + NEAR)],
        [
            shape_of(*grid.shape, dtype=FL), shape_of(pairs, full), shape_of(pairs, half),
            *slab_shapes(OWNER_BLOCKS * rows, half),
        ],
        [
            pltpu.VMEM((NEAR * OWNER_BLOCKS, rows, full), BF),
            pltpu.VMEM((NEAR * OWNER_BLOCKS, rows, half), FL),
        ],
    )(pair_mesh, pair_count, interp, grid, cotangent, w_dec, *near)


def outer(pair_count, y, dz, made):
    pairs, full = y.shape
    half = dz.shape[1]
    cost = pl.CostEstimate(
        flops=2 * pairs * full * half, bytes_accessed=2 * pairs * (full + half), transcendentals=0
    )
    outs = [shape_of(half, full, dtype=FL), shape_of(*made.shape)]
    return held(outer_kernel, [SMEM, *[VMEM] * 3], outs, cost=cost)(pair_count, y, dz, made)


def encoder_grad(pair_mesh, pair_count, x_own, x_other, slope, near, grad_dec):
    half = slope.shape[1]
    rows = near[0].shape[1] // OWNER_BLOCKS
    return held(
        encoder_grad_kernel,
        [SMEM, SMEM, *[VMEM] * (4 + NEAR)],
        shape_of(8 * half, half // 2),
        [pltpu.VMEM((NEAR * OWNER_BLOCKS, rows, half), BF), pltpu.VMEM((2, half, half), FL)],
    )(pair_mesh, pair_count, x_own, x_other, slope, *near, grad_dec)


def local(grid, interp, mesh_init, w_enc, w_dec, cotangent, pair_mesh, pair_count):
    full, half = w_enc.shape
    pair_mesh = pair_mesh.T
    swapped = [swap(value) for value in (grid, mesh_init, w_dec)]
    grid_other, mesh_other, w_dec_other = lax.optimization_barrier(swapped)
    mesh_both = jnp.stack([mesh_init, mesh_other])

    interp, w_enc, x_own, pair_mesh, pair_count = lift_own(interp, grid, w_enc, pair_mesh, pair_count)
    x_other, own, mine, other = encode(pair_mesh, pair_count, interp, w_enc, x_own, grid_other)
    slope = slopes(pair_count, w_enc, x_own, x_other)
    sums, got, slope = reduce_to_owner(own, mine, other, slope)
    agg = sums.astype(FL) + got.astype(FL)[::-1]
    mesh_lat = (mesh_both.astype(FL) + 0.25 * agg).astype(BF)
    near = spread_from_owner(mesh_lat)

    out, y, dz, own, mine, other = decode(
        pair_mesh, pair_count, interp, grid, cotangent, w_dec, near
    )
    sums, got, (grad_dec, out) = reduce_to_owner(own, mine, other, outer(pair_count, y, dz, out))
    grad_mesh = simple(mesh_grad_kernel, shape_of(*sums.shape))(sums, got, w_dec, w_dec_other)
    near = spread_from_owner(grad_mesh, lambda part: part[0])
    flat = encoder_grad(pair_mesh, pair_count, x_own, x_other, slope, near, grad_dec)

    plane, line = plane_groups(lax.axis_size("band"))
    across = len(plane[0])
    chunks = exchange(flat.reshape(across, -1, half // 2), plane)
    piece = simple(sum_kernel, shape_of(len(line[0]), *chunks.shape[1:]))(chunks)
    pieces = exchange(piece, line)
    spread = simple(sum_kernel, shape_of(*chunks.shape))(pieces)
    flat = exchange(spread, plane).reshape(flat.shape)
    grads = [shape_of(full, half, dtype=FL)] * 2
    grad_enc, grad_dec = simple(finish_kernel, grads)(flat)
    return (out, grad_enc, grad_dec)


def solution(mesh):
    placed = (
        P("band", "mp"),
        P("band", None, None, None),
        P("band", "mp"),
        P(None, "mp"),
        P(None, "mp"),
        P("band", "mp"),
        P("band", None),
        P("band"),
    )
    return jax.shard_map(
        local,
        mesh=mesh,
        in_specs=placed,
        out_specs=(P("band", "mp"), P(None, "mp"), P(None, "mp")),
        check_vma=False,
    )
```
